512 devices in a mesh: tok: 32 (over z_lo, y), lat: 16 (over x, z_hi, core).
Axes of the slice: x: 4, y: 8, z: 8 (z_hi: 2, z_lo: 4; z = z_hi * 4 + z_lo), core: 2. Of those that a mesh axis runs over, the one named last changes fastest.
Arguments:
- resid: bfloat16 [128, 3584], P('tok'), may hold values from -6 to 6
- enc_weight: bfloat16 [49152, 3584], P(('tok', 'lat')), may hold values from -0.09375 to 0.09375
- enc_bias: float32 [49152], P(('tok', 'lat')), may hold values from -3 to 3
- decoder_weight_matrix: bfloat16 [49152, 3584], P(('tok', 'lat')), may hold values from -0.109375 to 0.109375
- decoder_bias_vector: float32 [3584], replicated, may hold values from -3 to 3
- norm_gain: float32 [3584], replicated, may hold values from 0.1 to 1.9
- unembed: bfloat16 [131072, 3584], P(('tok', 'lat')), may hold values from -0.3125 to 0.3125
- orig_logits: bfloat16 [128, 131072], P(None, ('tok', 'lat')), may hold values from -24 to 24
Outputs:
- grad_enc: bfloat16 [49152, 3584], P(('tok', 'lat'))
- grad_dec: bfloat16 [49152, 3584], P(('tok', 'lat'))
- encoder_bias_gradient: float32 [49152], P(('tok', 'lat'))
- grad_bdec: float32 [3584], replicated
- kl_rows: float32 [128], replicated
The draws below stay inside these ranges and needn't reach their ends.
All inputs are finite; a program needn't handle non-finite values.
Results may differ from the reference program's by a relative error of at most 0.015.
Values may be sent and summed in bfloat16 or wider, within the bound.
A program may use at most 64 MiB of HBM per device.

```python
import jax
import jax.numpy as jnp
from jax import lax

D = 3584
L = 49152
V = 131072
TOKENS = 128


def spiked(result, key, source, target, shards_of, factor):
    def block_of(dim):
        return (jnp.arange(result.shape[dim]) // (result.shape[dim] // shards_of)).reshape((-1,) + (1,) * (result.ndim - 1 - dim))

    one_side = jax.random.permutation(key, shards_of)[block_of(target)]
    far = (block_of(target) + shards_of // 2) % shards_of
    return jnp.where((block_of(source) == one_side) | (block_of(source) == far), factor * result, result)


def shard_levels(stream_key, extent, cuts, smallest, top_value):
    level, own = 1.0, jax.random.fold_in(stream_key, 6)
    for dim, shards_of in cuts:
        steps = jnp.exp(jax.random.uniform(jax.random.fold_in(own, dim), (shards_of,), jnp.float32, smallest / len(cuts), top_value / len(cuts)))
        level = level * jnp.repeat(steps, extent[dim] // shards_of).reshape([-1 if axis == dim else 1 for axis in range(len(extent))])
    return level


def centred(stream_key, extent, spread, reach, shards=(), held_as=jnp.bfloat16):
    entries = spread * jax.random.normal(stream_key, extent, jnp.float32)
    if shards:
        entries = entries * shard_levels(stream_key, extent, shards, -0.22, 0.18)
    return jnp.clip(entries, -reach, reach).astype(held_as)


def heavy_noise(stream_key, extent, spread, most, shards, heavy, held_as=jnp.bfloat16):
    entries = spread * jax.random.normal(stream_key, extent, jnp.float32)
    if shards:
        entries = entries * shard_levels(stream_key, extent, shards, -0.22, 0.18)
    return jnp.clip(spiked(entries, jax.random.fold_in(stream_key, 3), *heavy), -most, most).astype(held_as)


def setup_inputs(seed: int = 0) -> dict:
    key_of = jax.random.split(jax.random.key(seed), 9)
    resid = centred(key_of[0], (TOKENS, D), 1.0, 6.0, ((0, 32),))
    enc_weight = centred(key_of[1], (L, D), D ** -0.5, 0.09375, ((0, 512),))
    enc_bias = centred(key_of[2], (L,), 0.5, 3.0, ((0, 512),), jnp.float32)
    decoder_weight_matrix = heavy_noise(key_of[3], (L, D), L ** -0.5, 0.109375, ((0, 512),), (0, 1, 512, 6.0))
    decoder_bias_vector = centred(key_of[4], (D,), 0.5, 3.0, (), jnp.float32)
    norm_gain = jnp.clip(1.0 + 0.18 * jax.random.normal(key_of[5], (D,), jnp.float32), 0.1, 1.9)
    unembed = centred(key_of[6], (V, D), (D // 9) ** -0.5, 0.3125, ((0, 512),))
    orig_logits = centred(key_of[7], (TOKENS, V), 3.0, 24.0, ((1, 512),))
    return dict(resid=resid, enc_weight=enc_weight, enc_bias=enc_bias, decoder_weight_matrix=decoder_weight_matrix, decoder_bias_vector=decoder_bias_vector, norm_gain=norm_gain, unembed=unembed, orig_logits=orig_logits)


def reference(resid, enc_weight, enc_bias, decoder_weight_matrix, decoder_bias_vector, norm_gain, unembed, orig_logits):
    xin = (resid.astype(jnp.float32) - decoder_bias_vector).astype(jnp.bfloat16)
    pre = jnp.dot(xin, enc_weight.T, preferred_element_type=jnp.float32) + enc_bias
    latent_activations = (jax.nn.softplus(4.0 * pre) / 4.0).astype(jnp.bfloat16)
    estimated_input = (jnp.dot(latent_activations, decoder_weight_matrix, preferred_element_type=jnp.float32) + decoder_bias_vector).astype(jnp.bfloat16)
    complete_input_rows = estimated_input.astype(jnp.float32)
    rinv = lax.rsqrt(lax.optimization_barrier(jnp.mean(complete_input_rows * complete_input_rows, axis=1, keepdims=True)) + 1e-06)
    normed = (complete_input_rows * rinv * norm_gain).astype(jnp.bfloat16)
    capped = 30.0 * jnp.tanh(jnp.dot(normed, unembed.T, preferred_element_type=jnp.float32) / 30.0)
    orig = orig_logits.astype(jnp.float32)
    exp_model = jnp.exp(capped)
    exp_orig = jnp.exp(orig)
    total_model = lax.optimization_barrier(jnp.sum(exp_model, axis=1))
    total_orig = lax.optimization_barrier(jnp.sum(exp_orig, axis=1))
    log_orig = orig - jnp.log(total_orig)[:, None]
    log_model = capped - jnp.log(total_model)[:, None]
    kl_rows = lax.optimization_barrier(jnp.sum(exp_orig / total_orig[:, None] * (log_orig - log_model), axis=1))
    dcap = exp_model / total_model[:, None] - exp_orig / total_orig[:, None]
    dz = (dcap * (1.0 - (capped / 30.0) ** 2)).astype(jnp.bfloat16)
    dnormed = jnp.dot(dz, unembed, preferred_element_type=jnp.float32)
    scaled = dnormed * norm_gain
    dxhat = rinv * (scaled - complete_input_rows * rinv * rinv * lax.optimization_barrier(jnp.mean(complete_input_rows * scaled, axis=1, keepdims=True)))
    dxhat_low = dxhat.astype(jnp.bfloat16)
    grad_dec = jnp.dot(latent_activations.T, dxhat_low, preferred_element_type=jnp.float32).astype(jnp.bfloat16)
    dpre = jnp.dot(dxhat_low, decoder_weight_matrix.T, preferred_element_type=jnp.float32) * jax.nn.sigmoid(4.0 * pre)
    dpre_low = dpre.astype(jnp.bfloat16)
    grad_enc = jnp.dot(dpre_low.T, xin, preferred_element_type=jnp.float32).astype(jnp.bfloat16)
    encoder_bias_gradient = lax.optimization_barrier(jnp.sum(dpre, axis=0))
    through = jnp.dot(encoder_bias_gradient, enc_weight.astype(jnp.float32), precision=lax.Precision.HIGHEST)
    grad_bdec = lax.optimization_barrier(jnp.sum(dxhat, axis=0)) - through
    return (grad_enc, grad_dec, encoder_bias_gradient, grad_bdec, kl_rows)
```

```python
import jax
import jax.numpy as jnp
from jax import lax
from jax.experimental import pallas as pl
from jax.experimental.pallas import tpu as pltpu
from jax.sharding import PartitionSpec as P

MESH = pl.DeviceIdType.MESH
F32, BF16 = jnp.float32, jnp.bfloat16
D, ROWS, LAT, VOC = 3584, 128, 96, 256
HALF = D // 2
NT = (((1,), (1,)), ((), ()))
TN = (((0,), (0,)), ((), ()))
N_SEMS = 140


def dot(a, b, dims=(((1,), (0,)), ((), ())), precision=None):
    return lax.dot_general(a, b, dims, preferred_element_type=F32, precision=precision)


def kernel(
    resid_ref, enc_hbm, encb_ref, dec_hbm, decb_ref, gain_ref, unemb_hbm, orig_ref,
    genc_hbm, gdec_hbm, ebg_ref, gbd_ref, kl_ref,
    enc, dec, unemb, genc, gdec,
    zx, xf, xi, p_own, acc,
    core_out, core_in, xs, xr, zs, zr, ye, xh,
    core_out2, core_in2, xs2, xr2, zs2, zr2, ye2, dn,
    dz, eo, olog, sig, acts_ref, dxl, brow,
    small_c, small_x, small_z, small_y,
    th, th_c, th_x, th_z, th_y, th_all,
    local_sems, ss, rs,
):
    t, l = lax.axis_index("tok"), lax.axis_index("lat")
    zlo, y = lax.div(t, 8), lax.rem(t, 8)
    x, zhi, core = lax.div(l, 4), lax.rem(lax.div(l, 2), 2), lax.rem(l, 2)
    z = zhi * 4 + zlo
    other = 1 - core

    def device(x, y, z, c):
        return (lax.rem(z, 4) * 8 + y, x * 4 + lax.div(z, 4) * 2 + c)

    def on_core():
        return device(x, y, z, other)

    def on_x(k):
        return device(lax.rem(x + k, 4), y, z, core)

    def on_y(k):
        return device(x, lax.rem(y + k, 8), z, core)

    def on_z(k):
        return device(x, y, lax.rem(z + k, 8), core)

    counter = [0]
    sent = []

    def send(src, dst, target):
        i = counter[0]
        counter[0] += 1
        copy = pltpu.make_async_remote_copy(
            src_ref=src, dst_ref=dst, send_sem=ss.at[i], recv_sem=rs.at[i],
            device_id=target, device_id_type=MESH,
        )
        copy.start()
        sent.append(copy)
        return copy

    loads = []
    for i, (src, dst) in enumerate(((enc_hbm, enc), (dec_hbm, dec), (unemb_hbm, unemb))):
        copy = pltpu.make_async_copy(src, dst, local_sems.at[i])
        copy.start()
        loads.append(copy)

    barrier = pltpu.get_barrier_semaphore()
    partners = [on_core()] + [on_x(k) for k in (1, 2, 3)]
    partners += [on_y(k) for k in range(1, 8)] + [on_z(k) for k in range(1, 8)]
    for target in partners:
        pl.semaphore_signal(barrier, inc=1, device_id=target, device_id_type=MESH)

    piece = x * 2 + core
    start = pl.multiple_of(jnp.minimum(piece, 6) * 512, 512)
    mine = resid_ref[:, pl.ds(start, 512)].astype(F32) - decb_ref[:, pl.ds(start, 512)]
    zx[zlo, 0:4, :] = mine
    zx[zlo, 4:8, :] = mine
    acc[...] = jnp.zeros_like(acc)
    zs[...] = jnp.zeros_like(zs)
    zs2[...] = jnp.zeros_like(zs2)
    pl.semaphore_wait(barrier, len(partners))

    copies = [send(zx.at[zlo], zx.at[zlo], on_z(k)) for k in (1, 7, 2)]
    row = lax.broadcasted_iota(jnp.int32, (ROWS, ROWS), 0)
    col = lax.broadcasted_iota(jnp.int32, (ROWS, ROWS), 1)
    source = ((row >> 2) & 3) * 32 + (row >> 4) * 4 + (row & 3)
    perm = jnp.where(col == source, 1.0, 0.0).astype(F32)
    o = dot(perm.astype(BF16), orig_ref[...])
    olog[...] = o
    eo[...] = jnp.exp(o)
    for copy in copies:
        copy.wait_recv()
    for k in range(4):
        xf[4 * k : 4 * k + 4, :] = zx[k, 0:4, :]
    rows_y = pl.ds(pl.multiple_of(y * 16, 16), 16)
    cols_q = pl.ds(pl.multiple_of(piece * 512, 512), 512)
    xi[rows_y, cols_q] = xf[...].astype(BF16)
    block = xi.at[rows_y, cols_q]
    copies = [send(block, block, on_y(k)) for k in range(1, 8)]
    for copy in copies:
        copy.wait_recv()
    block = xi.at[:, cols_q]
    copies = [send(block, block, on_x(k)) for k in (1, 2, 3)]
    forwards = [send(block, block, on_core())]
    loads[0].wait()
    for k, copy in zip((1, 2, 3), copies):
        copy.wait_recv()
        q = lax.rem(x - k + 4, 4) * 2 + core
        block = xi.at[:, pl.ds(pl.multiple_of(q * 512, 512), 512)]
        forwards.append(send(block, block, on_core()))
    for copy in forwards:
        copy.wait_recv()

    def enc_step(j, total):
        cols = pl.ds(pl.multiple_of(j * 512, 512), 512)
        return total + dot(xi[:, cols], enc[:, cols], NT)

    pre = lax.fori_loop(0, 7, enc_step, jnp.zeros((ROWS, LAT), F32)) + encb_ref[...]
    four = 4.0 * pre
    acts = (jnp.maximum(four, 0.0) + jnp.log1p(jnp.exp(-jnp.abs(four)))) * 0.25
    acts = acts.astype(BF16)
    sig[...] = jax.nn.sigmoid(four)
    acts_ref[...] = acts

    rows_x = pl.ds(pl.multiple_of(x * 32, 32), 32)
    cols_z = pl.ds(pl.multiple_of(z * 256, 256), 256)

    def all_reduce(term, core_out, core_in, xs, xr, zs, zr, ye, full, bias):
        def fill_out(j, _):
            cols = pl.ds(pl.multiple_of(j * 256, 256), 256)
            core_out[:, cols] = term(other, j).astype(BF16)
            return 0

        lax.fori_loop(0, 7, fill_out, 0)
        copy = send(core_out, core_in, on_core())

        def fill_own(j, _):
            p_own[:, pl.ds(pl.multiple_of(j * 256, 256), 256)] = term(core, j)
            return 0

        lax.fori_loop(0, 7, fill_own, 0)
        copy.wait_recv()

        def add_core(j, _):
            cols = pl.ds(pl.multiple_of(j * 256, 256), 256)
            s = p_own[:, cols] + core_in[:, cols].astype(F32)
            p_own[:, cols] = s
            xs[:, cols] = s.astype(BF16)
            return 0

        lax.fori_loop(0, 7, add_core, 0)
        copies = []
        for k in (1, 2, 3):
            there = pl.ds(pl.multiple_of(lax.rem(x + k, 4) * 32, 32), 32)
            copies.append(send(xs.at[there, :], xr.at[k - 1], on_x(k)))
        for copy in copies:
            copy.wait_recv()

        def add_x(j, _):
            cols = pl.ds(pl.multiple_of(j * 256, 256), 256)
            s = p_own[rows_x, cols]
            for k in range(3):
                s = s + xr[k, :, cols].astype(F32)
            acc[:, cols] = s
            zs[:, cols] = s.astype(BF16)
            return 0

        lax.fori_loop(0, 7, add_x, 0)
        copies = []
        for k in range(1, 8):
            there = pl.ds(pl.multiple_of(lax.rem(z + k, 8) * 256, 256), 256)
            copies.append(send(zs.at[:, there], zr.at[k - 1], on_z(k)))
        for copy in copies:
            copy.wait_recv()
        s = acc[:, cols_z]
        for k in range(7):
            s = s + zr[k].astype(F32)
        ye[y] = s.astype(BF16)
        copies = [send(ye.at[y], ye.at[y], on_y(k)) for k in range(1, 8)]
        for copy in copies:
            copy.wait_recv()
        s = ye[0].astype(F32)
        for k in range(1, 8):
            s = s + ye[k].astype(F32)
        if bias is not None:
            begin = pl.multiple_of(core * HALF + jnp.minimum(z, 6) * 256, 256)
            s = s + bias[:, pl.ds(begin, 256)]
        full[core, rows_x, cols_z] = s.astype(BF16)
        block = full.at[core, rows_x, cols_z]
        copies = [send(block, block, on_z(k)) for k in range(1, 8)]
        for copy in copies:
            copy.wait_recv()
        block = full.at[core, rows_x, :]
        copies = [send(block, block, on_x(k)) for k in (1, 2, 3)]
        forwards = [send(block, block, on_core())]
        for k, copy in zip((1, 2, 3), copies):
            copy.wait_recv()
            here = pl.ds(pl.multiple_of(lax.rem(x - k + 4, 4) * 32, 32), 32)
            block = full.at[core, here, :]
            forwards.append(send(block, block, on_core()))
        for copy in forwards:
            copy.wait_recv()

    loads[1].wait()

    def recon_term(half, j):
        return dot(acts_ref[...], dec[:, pl.ds(pl.multiple_of(half * HALF + j * 256, 256), 256)])

    all_reduce(recon_term, core_out, core_in, xs, xr, zs, zr, ye, xh, decb_ref)

    squares = jnp.zeros((ROWS, 256), F32)
    for half in range(2):
        def square_step(j, total, half=half):
            v = xh[half, :, pl.ds(pl.multiple_of(j * 256, 256), 256)].astype(F32)
            return total + v * v

        squares = lax.fori_loop(0, 7, square_step, squares)
    rinv = lax.rsqrt(jnp.sum(squares, axis=1, keepdims=True) * (1.0 / D) + 1e-06)
    loads[2].wait()
    raw = jnp.zeros((ROWS, VOC), F32)
    for half in range(2):
        def logit_step(j, total, half=half):
            cols = pl.ds(pl.multiple_of(half * HALF + j * 256, 256), 256)
            v = xh[half, :, pl.ds(pl.multiple_of(j * 256, 256), 256)].astype(F32)
            normed = (v * rinv * gain_ref[:, cols]).astype(BF16)
            return total + dot(normed, unemb[:, cols], NT)

        raw = lax.fori_loop(0, 7, logit_step, raw)
    shape = jnp.tanh(raw * (1.0 / 30.0))
    capped = 30.0 * shape
    exp_model = jnp.exp(capped)
    exp_orig = eo[...]

    lane = lax.broadcasted_iota(jnp.int32, (ROWS, ROWS), 1)
    sums = jnp.where(lane == 0, jnp.sum(exp_model, axis=1, keepdims=True), 0.0)
    sums = jnp.where(lane == 1, jnp.sum(exp_orig, axis=1, keepdims=True), sums)
    sums = jnp.where(
        lane == 2, jnp.sum(exp_orig * (olog[...] - capped), axis=1, keepdims=True), sums
    )
    s = sums.T[0:8, :]

    def exchange(buffer, value, here, count, target):
        buffer[here] = value
        copies = [send(buffer.at[here], buffer.at[here], target(k)) for k in range(1, count)]
        for copy in copies:
            copy.wait_recv()
        total = buffer[0]
        for k in range(1, count):
            total = total + buffer[k]
        return total

    s = exchange(small_c, s, core, 2, lambda k: on_core())
    s = exchange(small_x, s, x, 4, on_x)
    s = exchange(small_z, s, z, 8, on_z)
    s = exchange(small_y, s, y, 8, on_y)
    kl = s[2:3] / s[1:2] - jnp.log(s[1:2]) + jnp.log(s[0:1])
    kl_ref[...] = dot(jnp.broadcast_to(kl, (8, ROWS)), perm, precision=lax.Precision.HIGHEST)
    columns = jnp.concatenate([s, jnp.zeros((ROWS - 8, ROWS), F32)], axis=0).T
    dcap = exp_model * (1.0 / columns[:, 0:1]) - exp_orig * (1.0 / columns[:, 1:2])
    dz[...] = (dcap * (1.0 - shape * shape)).astype(BF16)

    def grad_term(half, j):
        return dot(dz[...], unemb[:, pl.ds(pl.multiple_of(half * HALF + j * 256, 256), 256)])

    all_reduce(grad_term, core_out2, core_in2, xs2, xr2, zs2, zr2, ye2, dn, None)

    dots = jnp.zeros((ROWS, 256), F32)
    for half in range(2):
        def mean_step(j, total, half=half):
            cols = pl.ds(pl.multiple_of(j * 256, 256), 256)
            gain = gain_ref[:, pl.ds(pl.multiple_of(half * HALF + j * 256, 256), 256)]
            return total + xh[half, :, cols].astype(F32) * (dn[half, :, cols].astype(F32) * gain)

        dots = lax.fori_loop(0, 7, mean_step, dots)
    factor = jnp.sum(dots, axis=1, keepdims=True) * (1.0 / D) * rinv * rinv
    back = jnp.zeros((ROWS, LAT), F32)
    for half in range(2):
        def back_step(j, total, half=half):
            cols = pl.ds(pl.multiple_of(j * 256, 256), 256)
            whole = pl.ds(pl.multiple_of(half * HALF + j * 256, 256), 256)
            scaled = dn[half, :, cols].astype(F32) * gain_ref[:, whole]
            dxhat = rinv * (scaled - xh[half, :, cols].astype(F32) * factor)
            brow[:, whole] = jnp.sum(dxhat, axis=0, keepdims=True)
            rounded = dxhat.astype(BF16)
            dxl[:, whole] = rounded
            return total + dot(rounded, dec[:, whole], NT)

        back = lax.fori_loop(0, 7, back_step, back)
    dpre = back * sig[...]
    ebg = jnp.sum(dpre, axis=0, keepdims=True)
    ebg_ref[...] = ebg

    high = ebg.astype(BF16).astype(F32)
    middle = (ebg - high).astype(BF16).astype(F32)
    last = ebg - high - middle
    stacked = jnp.concatenate([high, middle, last, jnp.zeros((13, LAT), F32)], axis=0).astype(BF16)
    for j in range(7):
        part = dot(stacked, enc[:, 512 * j : 512 * j + 512])
        th[j : j + 1, :] = part[0:1] + part[1:2] + part[2:3]
    th[7:8, :] = jnp.zeros((1, 512), F32)
    here = pl.ds(pl.multiple_of(core * 256, 256), 256)
    there = pl.ds(pl.multiple_of(other * 256, 256), 256)
    copy = send(th.at[:, there], th_c, on_core())
    acts_t = acts_ref[...].astype(F32).T.astype(BF16)
    dpre_t = dpre.T.astype(BF16)
    copy.wait_recv()
    total = th[:, here] + th_c[...]
    th_x[x] = total
    copies = [send(th_x.at[x], th_x.at[x], on_x(k)) for k in (1, 2, 3)]

    def dec_step(j, _):
        cols = pl.ds(pl.multiple_of(j * 512, 512), 512)
        gdec[:, cols] = dot(acts_t, dxl[:, cols]).astype(BF16)
        return 0

    lax.fori_loop(0, 7, dec_step, 0)
    store_dec = pltpu.make_async_copy(gdec, gdec_hbm, local_sems.at[3])
    store_dec.start()
    for copy in copies:
        copy.wait_recv()
    total = th_x[0]
    for k in range(1, 4):
        total = total + th_x[k]
    th_z[z] = total
    copies = [send(th_z.at[z], th_z.at[z], on_z(k)) for k in range(1, 8)]

    def enc_grad_step(j, _):
        cols = pl.ds(pl.multiple_of(j * 512, 512), 512)
        genc[:, cols] = dot(dpre_t, xi[:, cols]).astype(BF16)
        return 0

    lax.fori_loop(0, 7, enc_grad_step, 0)
    store_enc = pltpu.make_async_copy(genc, genc_hbm, local_sems.at[4])
    store_enc.start()
    for copy in copies:
        copy.wait_recv()
    total = th_z[0]
    for k in range(1, 8):
        total = total + th_z[k]
    total = exchange(th_y, total, y, 8, on_y)
    th_all[:, here] = total
    copy = send(th_all.at[:, here], th_all.at[:, here], on_core())
    copy.wait_recv()
    for j in range(7):
        gbd_ref[j : j + 1, :] = brow[:, 512 * j : 512 * j + 512] - th_all[j : j + 1, :]
    gbd_ref[7:8, :] = jnp.zeros((1, 512), F32)
    for copy in sent:
        copy.wait_send()
    store_dec.wait()
    store_enc.wait()


def per_device(resid, enc_weight, enc_bias, dec_weight, dec_bias, norm_gain, unembed, orig_logits):
    vmem = pl.BlockSpec(memory_space=pltpu.VMEM)
    hbm = pl.BlockSpec(memory_space=pl.ANY)
    reduce_scratch = [
        pltpu.VMEM((ROWS, HALF), BF16),
        pltpu.VMEM((ROWS, HALF), BF16),
        pltpu.VMEM((ROWS, HALF), BF16),
        pltpu.VMEM((3, 32, HALF), BF16),
        pltpu.VMEM((32, 2048), BF16),
        pltpu.VMEM((7, 32, 256), BF16),
        pltpu.VMEM((8, 32, 256), BF16),
        pltpu.VMEM((2, ROWS, 2048), BF16),
    ]
    genc, gdec, ebg, gbd, kl = pl.pallas_call(
        kernel,
        out_shape=(
            jax.ShapeDtypeStruct((LAT, D), BF16),
            jax.ShapeDtypeStruct((LAT, D), BF16),
            jax.ShapeDtypeStruct((1, LAT), F32),
            jax.ShapeDtypeStruct((8, 512), F32),
            jax.ShapeDtypeStruct((8, ROWS), F32),
        ),
        in_specs=[vmem, hbm, vmem, hbm, vmem, vmem, hbm, vmem],
        out_specs=(hbm, hbm, vmem, vmem, vmem),
        scratch_shapes=[
            pltpu.VMEM((LAT, D), BF16),
            pltpu.VMEM((LAT, D), BF16),
            pltpu.VMEM((VOC, D), BF16),
            pltpu.VMEM((LAT, D), BF16),
            pltpu.VMEM((LAT, D), BF16),
            pltpu.VMEM((4, 8, 512), F32),
            pltpu.VMEM((16, 512), F32),
            pltpu.VMEM((ROWS, 4096), BF16),
            pltpu.VMEM((ROWS, HALF), F32),
            pltpu.VMEM((32, 2048), F32),
            *reduce_scratch,
            *reduce_scratch,
            pltpu.VMEM((ROWS, VOC), BF16),
            pltpu.VMEM((ROWS, VOC), F32),
            pltpu.VMEM((ROWS, VOC), F32),
            pltpu.VMEM((ROWS, LAT), F32),
            pltpu.VMEM((ROWS, LAT), BF16),
            pltpu.VMEM((ROWS, D), BF16),
            pltpu.VMEM((1, D), F32),
            *(pltpu.VMEM((n, 8, ROWS), F32) for n in (2, 4, 8, 8)),
            pltpu.VMEM((8, 512), F32),
            pltpu.VMEM((8, 256), F32),
            *(pltpu.VMEM((n, 8, 256), F32) for n in (4, 8, 8)),
            pltpu.VMEM((8, 512), F32),
            pltpu.SemaphoreType.DMA((5,)),
            pltpu.SemaphoreType.DMA((N_SEMS,)),
            pltpu.SemaphoreType.DMA((N_SEMS,)),
        ],
        compiler_params=pltpu.CompilerParams(
            collective_id=0, has_side_effects=True, vmem_limit_bytes=40 * 2**20
        ),
        cost_estimate=pl.CostEstimate(flops=10**9, bytes_accessed=5 * 10**6, transcendentals=0),
        name="train_step",
    )(
        resid, enc_weight, enc_bias.reshape(1, LAT), dec_weight, dec_bias.reshape(1, D),
        norm_gain.reshape(1, D), unembed, orig_logits,
    )
    return genc, gdec, ebg.reshape(LAT), gbd[:7].reshape(D), kl[0]


def solution(mesh):
    split = P(("tok", "lat"), None)
    return jax.shard_map(
        per_device,
        mesh=mesh,
        in_specs=(
            P("tok", None), split, P(("tok", "lat")), split, P(), P(), split,
            P(None, ("tok", "lat")),
        ),
        out_specs=(split, split, P(("tok", "lat")), P(), P()),
        check_vma=False,
    )
```

```python
import jax
import jax.numpy as jnp
from jax import lax
from jax.experimental import pallas as pl
from jax.experimental.pallas import tpu as pltpu
from jax.sharding import PartitionSpec as P

MESH = pl.DeviceIdType.MESH
F32, BF16 = jnp.float32, jnp.bfloat16
D, ROWS, LAT, VOC = 3584, 128, 96, 256
HALF = D // 2
CHAIN = ROWS // 2
NN = (((1,), (0,)), ((), ()))
NT = (((1,), (1,)), ((), ()))
N_SEMS = 280


def dot(a, b, dims=NN, precision=None):
    return lax.dot_general(a, b, dims, preferred_element_type=F32, precision=precision)


def block_of(index, size):
    return pl.ds(pl.multiple_of(index * size, size), size)


def kernel(
    resid_ref, enc_hbm, encb_hbm, dec_hbm, decb_hbm, gain_hbm, unemb_hbm, orig_hbm,
    genc_hbm, gdec_hbm, ebg_ref, gbd_ref, kl_ref,
    enc, dec, unemb, encb, decb, gain_ref, orig, genc, gdec,
    zx, xf, xi, p_own, acc,
    core_out, core_in, xs, xr, zs, zr, ye, xh,
    core_out2, core_in2, xs2, xr2, zs2, zr2, ye2, dn,
    eo, olog, sig, acts_ref, dxl, brow,
    small_x, small_z, small_y,
    th, th_c, th_x, th_z, th_y, th_all,
    local_sems, ss, rs,
):
    t, l = lax.axis_index("tok"), lax.axis_index("lat")
    zlo, y = lax.div(t, 8), lax.rem(t, 8)
    x, zhi, core = lax.div(l, 4), lax.rem(lax.div(l, 2), 2), lax.rem(l, 2)
    z = zhi * 4 + zlo
    other = 1 - core

    def device(x, y, z, c):
        return (lax.rem(z, 4) * 8 + y, x * 4 + lax.div(z, 4) * 2 + c)

    def on_core():
        return device(x, y, z, other)

    def on_x(k):
        return device(lax.rem(x + k, 4), y, z, core)

    def on_xc(k, flip):
        return device(lax.rem(x + k, 4), y, z, other if flip else core)

    def on_y(k):
        return device(x, lax.rem(y + k, 8), z, core)

    def on_z(k):
        return device(x, y, lax.rem(z + k, 8), core)

    counter = [0]
    sent = []

    def send(src, dst, target):
        i = counter[0]
        counter[0] += 1
        copy = pltpu.make_async_remote_copy(
            src_ref=src, dst_ref=dst, send_sem=ss.at[i], recv_sem=rs.at[i],
            device_id=target, device_id_type=MESH,
        )
        copy.start()
        sent.append(copy)
        return copy

    def received(copies):
        for copy in copies:
            copy.wait_recv()

    def load(i, src, dst):
        copy = pltpu.make_async_copy(src, dst, local_sems.at[i])
        copy.start()
        return copy

    load_decb = load(0, decb_hbm, decb.at[0])
    load_orig = load(1, orig_hbm, orig)
    load_enc = load(2, enc_hbm, enc)
    load_encb = load(3, encb_hbm, encb.at[0])
    load_dec = load(4, dec_hbm, dec)
    load_gain = load(5, gain_hbm, gain_ref.at[0])
    load_unemb = load(6, unemb_hbm, unemb)

    barrier = pltpu.get_barrier_semaphore()
    partners = [on_core()] + [on_xc(k, flip) for k in (1, 2, 3) for flip in (False, True)]
    partners += [on_y(k) for k in range(1, 8)] + [on_z(k) for k in range(1, 8)]
    for target in partners:
        pl.semaphore_signal(barrier, inc=1, device_id=target, device_id_type=MESH)

    piece = x * 2 + core
    load_decb.wait()
    cols = pl.ds(pl.multiple_of(jnp.minimum(piece, 6) * 512, 512), 512)
    mine = resid_ref[:, cols].astype(F32) - decb[:, cols]
    zx[zlo, 0:4, :] = mine[:, 0:256]
    zx[zlo, 4:8, :] = mine[:, 256:512]
    for r in range(2):
        acc[r, :, HALF:2048] = jnp.zeros((16, 256), F32)
        zs[r, :, HALF:2048] = jnp.zeros((16, 256), BF16)
        zs2[r, :, HALF:2048] = jnp.zeros((16, 256), BF16)
    pl.semaphore_wait(barrier, len(partners))

    copies = [send(zx.at[zlo], zx.at[zlo], on_z(k)) for k in (2, 1, 7)]
    row = lax.broadcasted_iota(jnp.int32, (ROWS, ROWS), 0)
    col = lax.broadcasted_iota(jnp.int32, (ROWS, ROWS), 1)

    def natural(i):
        return ((i >> 2) & 3) * 32 + (i >> 4) * 4 + (i & 3)

    load_orig.wait()
    o = dot(jnp.where(col == natural(row), 1.0, 0.0).astype(BF16), orig[...])
    olog[...] = o
    eo[...] = jnp.exp(o)
    received(copies)
    for k in range(4):
        xf[4 * k : 4 * k + 4, 0:256] = zx[k, 0:4, :]
        xf[4 * k : 4 * k + 4, 256:512] = zx[k, 4:8, :]
    cols_q = block_of(piece, 512)
    rows_y = block_of(y, 16)
    xi[rows_y, cols_q] = xf[...].astype(BF16)
    block = xi.at[rows_y, cols_q]
    copies = {k: send(block, block, on_y(k)) for k in (4, 3, 5, 2, 6, 1, 7)}
    pieces = [[], [], []]

    def forward_rows(k):
        here = xi.at[block_of(lax.rem(y - k + 8, 8), 16), cols_q]
        for i in range(3):
            pieces[i].append(send(here, here, on_x(i + 1)))

    forward_rows(0)
    for k in (1, 7, 2, 6, 3, 5, 4):
        copies[k].wait_recv()
        forward_rows(k)
    block = xi.at[:, cols_q]
    forwards = [send(block, block, on_core())]
    for i in (0, 2, 1):
        received(pieces[i])
        q = lax.rem(x - (i + 1) + 4, 4) * 2 + core
        block = xi.at[:, block_of(q, 512)]
        forwards.append(send(block, block, on_core()))
    load_enc.wait()
    load_encb.wait()
    received(forwards)

    pre = encb[...]
    for j in range(7):
        cols = pl.ds(j * 512, 512)
        pre = pre + dot(xi[:, cols], enc[:, cols], NT)
    four = 4.0 * pre
    acts = (jnp.maximum(four, 0.0) + jnp.log1p(jnp.exp(-jnp.abs(four)))) * 0.25
    acts_ref[...] = acts.astype(BF16)
    sig[...] = jax.nn.sigmoid(four)
    load_dec.wait()

    cols_z = block_of(z, 256)

    def all_reduce(r, left, right, core_out, core_in, xs, xr, zs, zr, ye, full, bias):
        def term(half, j):
            return dot(left, right[:, pl.ds(pl.multiple_of(half * HALF + j * 256, 256), 256)])

        copies = []
        for begin, end in ((0, 4), (4, 7)):
            for j in range(begin, end):
                core_out[r, :, pl.ds(j * 256, 256)] = term(other, j).astype(BF16)
            cols = pl.ds(begin * 256, (end - begin) * 256)
            copies.append(send(core_out.at[r, :, cols], core_in.at[r, :, cols], on_core()))
        for j in range(7):
            p_own[r, :, pl.ds(j * 256, 256)] = term(core, j)
        yield
        received(copies)
        for j in range(7):
            cols = pl.ds(j * 256, 256)
            s = p_own[r, :, cols] + core_in[r, :, cols].astype(F32)
            p_own[r, :, cols] = s
            xs[r, :, cols] = s.astype(BF16)
        copies = []
        for k in (2, 1, 3):
            there = block_of(lax.rem(x + k, 4), 16)
            copies.append(send(xs.at[r, there, :], xr.at[r, k - 1], on_x(k)))
        yield
        received(copies)
        s = p_own[r, block_of(x, 16), :]
        for k in range(3):
            s = s + xr[r, k].astype(F32)
        acc[r, :, 0:HALF] = s
        zs[r, :, 0:HALF] = s.astype(BF16)
        copies = []
        for k in (4, 3, 5, 2, 6, 1, 7):
            there = block_of(lax.rem(z + k, 8), 256)
            copies.append(send(zs.at[r, :, there], zr.at[r, k - 1], on_z(k)))
        yield
        received(copies)
        s = acc[r, :, cols_z]
        for k in range(7):
            s = s + zr[r, k].astype(F32)
        ye[r, y] = s.astype(BF16)
        copies = [send(ye.at[r, y], ye.at[r, y], on_y(k)) for k in (4, 3, 5, 2, 6, 1, 7)]
        yield
        received(copies)
        s = ye[r, 0].astype(F32)
        for k in range(1, 8):
            s = s + ye[r, k].astype(F32)
        if bias is not None:
            begin = pl.multiple_of(core * HALF + jnp.minimum(z, 6) * 256, 256)
            s = s + bias[:, pl.ds(begin, 256)]
        rows_x = block_of(4 * r + x, 16)
        full[core, rows_x, cols_z] = s.astype(BF16)
        block = full.at[core, rows_x, cols_z]
        copies = [send(block, block, on_z(k)) for k in (4, 3, 5, 2, 6, 1, 7)]
        yield
        received(copies)
        block = full.at[core, rows_x, pl.ds(0, HALF)]
        copies = {k: send(block, block, on_x(k)) for k in (2, 1, 3)}
        forwards = [send(block, block, on_core())]
        yield
        for k in (1, 3, 2):
            copies[k].wait_recv()
            here = block_of(4 * r + lax.rem(x - k + 4, 4), 16)
            block = full.at[core, here, pl.ds(0, HALF)]
            forwards.append(send(block, block, on_core()))
        yield
        received(forwards)

    def exchange(buffer, value, here, count, target):
        buffer[here] = value
        order = [k for k in (4, 3, 5, 2, 6, 1, 7) if k < count]
        copies = [send(buffer.at[here], buffer.at[here], target(k)) for k in order]
        yield
        received(copies)
        total = buffer[0]
        for k in range(1, count):
            total = total + buffer[k]
        return total

    kls = [None, None]
    dpres = [None, None]

    def chain(r):
        rows = pl.ds(r * CHAIN, CHAIN)
        yield from all_reduce(
            r, acts_ref[rows, :], dec, core_out, core_in, xs, xr, zs, zr, ye, xh, decb
        )
        squares = jnp.zeros((CHAIN, 256), F32)
        for half in range(2):
            for j in range(7):
                v = xh[half, rows, pl.ds(j * 256, 256)].astype(F32)
                squares = squares + v * v
        rinv = lax.rsqrt(jnp.sum(squares, axis=1, keepdims=True) * (1.0 / D) + 1e-06)
        if r == 0:
            load_gain.wait()
            load_unemb.wait()
        raw = jnp.zeros((CHAIN, VOC), F32)
        for half in range(2):
            for j in range(7):
                cols = pl.ds(half * HALF + j * 256, 256)
                v = xh[half, rows, pl.ds(j * 256, 256)].astype(F32)
                normed = (v * rinv * gain_ref[:, cols]).astype(BF16)
                raw = raw + dot(normed, unemb[:, cols], NT)
        shape = jnp.tanh(raw * (1.0 / 30.0))
        capped = 30.0 * shape
        exp_model = jnp.exp(capped)
        exp_orig = eo[rows, :]

        lane = lax.broadcasted_iota(jnp.int32, (CHAIN, ROWS), 1)
        sums = jnp.where(lane == 0, jnp.sum(exp_model, axis=1, keepdims=True), 0.0)
        sums = jnp.where(lane == 1, jnp.sum(exp_orig, axis=1, keepdims=True), sums)
        cross = jnp.sum(exp_orig * (olog[rows, :] - capped), axis=1, keepdims=True)
        sums = jnp.where(lane == 2, cross, sums)
        s = jnp.concatenate([sums, jnp.zeros((CHAIN, ROWS), F32)], axis=0).T[0:4, :]
        here = x * 2 + core
        slot = small_x.at[r, here]
        slot[...] = s
        copies = [send(slot, slot, on_xc(k, f)) for k in (2, 1, 3, 0) for f in (True, False) if k or f]
        yield
        received(copies)
        s = small_x[r, 0]
        for k in range(1, 8):
            s = s + small_x[r, k]
        s = yield from exchange(small_z.at[r], s, z, 8, on_z)
        s = yield from exchange(small_y.at[r], s, y, 8, on_y)
        kls[r] = s[2:3] / s[1:2] - jnp.log(s[1:2]) + jnp.log(s[0:1])
        columns = jnp.concatenate([s, jnp.zeros((ROWS - 4, ROWS), F32)], axis=0).T[0:CHAIN, :]
        dcap = exp_model * (1.0 / columns[:, 0:1]) - exp_orig * (1.0 / columns[:, 1:2])
        dz = (dcap * (1.0 - shape * shape)).astype(BF16)
        yield from all_reduce(
            r, dz, unemb, core_out2, core_in2, xs2, xr2, zs2, zr2, ye2, dn, None
        )
        dots = jnp.zeros((CHAIN, 256), F32)
        for half in range(2):
            for j in range(7):
                cols = pl.ds(j * 256, 256)
                gain = gain_ref[:, pl.ds(half * HALF + j * 256, 256)]
                dots = dots + xh[half, rows, cols].astype(F32) * (dn[half, rows, cols].astype(F32) * gain)
        factor = jnp.sum(dots, axis=1, keepdims=True) * (1.0 / D) * rinv * rinv
        back = jnp.zeros((CHAIN, LAT), F32)
        for half in range(2):
            for j in range(7):
                cols = pl.ds(j * 256, 256)
                whole = pl.ds(half * HALF + j * 256, 256)
                scaled = dn[half, rows, cols].astype(F32) * gain_ref[:, whole]
                dxhat = rinv * (scaled - xh[half, rows, cols].astype(F32) * factor)
                brow[r, :, whole] = jnp.sum(dxhat, axis=0, keepdims=True)
                rounded = dxhat.astype(BF16)
                dxl[rows, whole] = rounded
                back = back + dot(rounded, dec[:, whole], NT)
        dpres[r] = back * sig[rows, :]

    running = [chain(0), chain(1)]
    while running:
        for generator in list(running):
            try:
                next(generator)
            except StopIteration:
                running.remove(generator)

    dpre = jnp.concatenate(dpres, axis=0)
    ebg = jnp.sum(dpre, axis=0, keepdims=True)
    ebg_ref[...] = ebg

    high = ebg.astype(BF16).astype(F32)
    middle = (ebg - high).astype(BF16).astype(F32)
    last = ebg - high - middle
    stacked = jnp.concatenate([high, middle, last, jnp.zeros((13, LAT), F32)], axis=0).astype(BF16)
    for j in range(7):
        part = dot(stacked, enc[:, 512 * j : 512 * j + 512])
        th[j : j + 1, :] = part[0:1] + part[1:2] + part[2:3]
    th[7:8, :] = jnp.zeros((1, 512), F32)
    here, there = block_of(core, 256), block_of(other, 256)
    copy = send(th.at[:, there], th_c, on_core())
    acts_t = acts_ref[...].astype(F32).T.astype(BF16)
    dpre_t = dpre.T.astype(BF16)
    copy.wait_recv()
    total = yield_through(exchange(th_x, th[:, here] + th_c[...], x, 4, on_x), lambda: None)

    def grad_dec():
        for j in range(7):
            cols = pl.ds(j * 512, 512)
            gdec[:, cols] = dot(acts_t, dxl[:, cols]).astype(BF16)

    def grad_enc():
        for j in range(7):
            cols = pl.ds(j * 512, 512)
            genc[:, cols] = dot(dpre_t, xi[:, cols]).astype(BF16)

    total = yield_through(exchange(th_z, total, z, 8, on_z), grad_dec)
    store_dec = load(7, gdec, gdec_hbm)
    exchange_y = exchange(th_y, total, y, 8, on_y)
    total = yield_through(exchange_y, grad_enc)
    store_enc = load(8, genc, genc_hbm)
    th_all[:, here] = total
    copy = send(th_all.at[:, here], th_all.at[:, here], on_core())
    rest = jnp.zeros((8, ROWS), F32)
    for r in range(2):
        perm = jnp.where((col == natural(row + CHAIN * r)) & (row < CHAIN), 1.0, 0.0)
        kl = jnp.where(lax.broadcasted_iota(jnp.int32, (8, ROWS), 1) < CHAIN, kls[r], 0.0)
        rest = rest + dot(kl, perm, precision=lax.Precision.HIGHEST)
    kl_ref[...] = rest
    copy.wait_recv()
    for j in range(7):
        cols = pl.ds(512 * j, 512)
        gbd_ref[:, cols] = brow[0, :, cols] + brow[1, :, cols] - th_all[j : j + 1, :]
    for copy in sent:
        copy.wait_send()
    store_dec.wait()
    store_enc.wait()


def yield_through(generator, meanwhile):
    next(generator)
    meanwhile()
    try:
        next(generator)
    except StopIteration as end:
        return end.value


def per_device(resid, enc_weight, enc_bias, dec_weight, dec_bias, norm_gain, unembed, orig_logits):
    vmem = pl.BlockSpec(memory_space=pltpu.VMEM)
    hbm = pl.BlockSpec(memory_space=pl.ANY)
    reduce_scratch = [
        pltpu.VMEM((2, CHAIN, HALF), BF16),
        pltpu.VMEM((2, CHAIN, HALF), BF16),
        pltpu.VMEM((2, CHAIN, HALF), BF16),
        pltpu.VMEM((2, 3, 16, HALF), BF16),
        pltpu.VMEM((2, 16, 2048), BF16),
        pltpu.VMEM((2, 7, 16, 256), BF16),
        pltpu.VMEM((2, 8, 16, 256), BF16),
        pltpu.VMEM((2, ROWS, 2048), BF16),
    ]
    genc, gdec, ebg, gbd, kl = pl.pallas_call(
        kernel,
        out_shape=(
            jax.ShapeDtypeStruct((LAT, D), BF16),
            jax.ShapeDtypeStruct((LAT, D), BF16),
            jax.ShapeDtypeStruct((1, LAT), F32),
            jax.ShapeDtypeStruct((1, D), F32),
            jax.ShapeDtypeStruct((8, ROWS), F32),
        ),
        in_specs=[vmem, hbm, hbm, hbm, hbm, hbm, hbm, hbm],
        out_specs=(hbm, hbm, vmem, vmem, vmem),
        scratch_shapes=[
            pltpu.VMEM((LAT, D), BF16),
            pltpu.VMEM((LAT, D), BF16),
            pltpu.VMEM((VOC, D), BF16),
            pltpu.VMEM((1, LAT), F32),
            pltpu.VMEM((1, D), F32),
            pltpu.VMEM((1, D), F32),
            pltpu.VMEM((ROWS, VOC), BF16),
            pltpu.VMEM((LAT, D), BF16),
            pltpu.VMEM((LAT, D), BF16),
            pltpu.VMEM((4, 8, 256), F32),
            pltpu.VMEM((16, 512), F32),
            pltpu.VMEM((ROWS, 4096), BF16),
            pltpu.VMEM((2, CHAIN, HALF), F32),
            pltpu.VMEM((2, 16, 2048), F32),
            *reduce_scratch,
            *reduce_scratch,
            pltpu.VMEM((ROWS, VOC), F32),
            pltpu.VMEM((ROWS, VOC), F32),
            pltpu.VMEM((ROWS, LAT), F32),
            pltpu.VMEM((ROWS, LAT), BF16),
            pltpu.VMEM((ROWS, D), BF16),
            pltpu.VMEM((2, 1, D), F32),
            *(pltpu.VMEM((2, 8, 4, ROWS), F32) for _ in range(3)),
            pltpu.VMEM((8, 512), F32),
            pltpu.VMEM((8, 256), F32),
            *(pltpu.VMEM((n, 8, 256), F32) for n in (4, 8, 8)),
            pltpu.VMEM((8, 512), F32),
            pltpu.SemaphoreType.DMA((9,)),
            pltpu.SemaphoreType.DMA((N_SEMS,)),
            pltpu.SemaphoreType.DMA((N_SEMS,)),
        ],
        compiler_params=pltpu.CompilerParams(
            collective_id=0, has_side_effects=True, vmem_limit_bytes=60 * 2**20
        ),
        cost_estimate=pl.CostEstimate(flops=10**9, bytes_accessed=5 * 10**6, transcendentals=0),
        name="train_step",
    )(resid, enc_weight, enc_bias, dec_weight, dec_bias, norm_gain, unembed, orig_logits)
    return genc, gdec, ebg.reshape(LAT), gbd.reshape(D), kl[0]


def solution(mesh):
    split = P(("tok", "lat"), None)
    return jax.shard_map(
        per_device,
        mesh=mesh,
        in_specs=(
            P("tok", None), split, P(("tok", "lat")), split, P(), P(), split,
            P(None, ("tok", "lat")),
        ),
        out_specs=(split, split, P(("tok", "lat")), P(), P()),
        check_vma=False,
    )
```

```python
import jax
import jax.numpy as jnp
from jax import lax
from jax.experimental import pallas as pl
from jax.experimental.pallas import tpu as pltpu
from jax.sharding import PartitionSpec as P

MESH = pl.DeviceIdType.MESH
F32, BF16 = jnp.float32, jnp.bfloat16
D, ROWS, LAT, VOC = 3584, 128, 96, 256
HALF = D // 2
CHAIN = ROWS // 2
NN = (((1,), (0,)), ((), ()))
NT = (((1,), (1,)), ((), ()))
N_SEMS = 240


def dot(a, b, dims=NN, precision=None):
    return lax.dot_general(a, b, dims, preferred_element_type=F32, precision=precision)


def block_of(index, size):
    return pl.ds(pl.multiple_of(index * size, size), size)


def kernel(
    resid_hbm, enc_hbm, encb_hbm, dec_hbm, decb_hbm, gain_hbm, unemb_hbm, orig_hbm,
    genc_hbm, gdec_hbm, ebg_hbm, gbd_hbm, kl_hbm,
    resid_ref, ebg_ref, gbd_ref, kl_ref,
    enc, dec, unemb, encb, decb, gain_ref, orig, genc, gdec,
    zx, xf, xi, p_own, acc,
    core_out, core_in, xs, xr, zs, zr, ye, xh,
    core_out2, core_in2, xs2, xr2, zs2, zr2, ye2, dn,
    eo, olog, sig, acts_ref, dxl, brow,
    small_x, small_z, small_y,
    th, th_c, th_x, th_z, th_y, th_all,
    local_sems, ss, rs,
):
    t, l = lax.axis_index("tok"), lax.axis_index("lat")
    zlo, y = lax.div(t, 8), lax.rem(t, 8)
    x, zhi, core = lax.div(l, 4), lax.rem(lax.div(l, 2), 2), lax.rem(l, 2)
    z = zhi * 4 + zlo
    other = 1 - core

    def device(x, y, z, c):
        return (lax.rem(z, 4) * 8 + y, x * 4 + lax.div(z, 4) * 2 + c)

    def on_core():
        return device(x, y, z, other)

    def on_x(k):
        return device(lax.rem(x + k, 4), y, z, core)

    def on_xc(k, flip):
        return device(lax.rem(x + k, 4), y, z, other if flip else core)

    def on_y(k):
        return device(x, lax.rem(y + k, 8), z, core)

    def on_z(k):
        return device(x, y, lax.rem(z + k, 8), core)

    counter = [0]
    sent = []

    def send(src, dst, target):
        i = counter[0]
        counter[0] += 1
        copy = pltpu.make_async_remote_copy(
            src_ref=src, dst_ref=dst, send_sem=ss.at[i], recv_sem=rs.at[i],
            device_id=target, device_id_type=MESH,
        )
        copy.start()
        sent.append(copy)
        return copy

    def group(target, whole):
        i = counter[0]
        counter[0] += 1

        def descriptor(block):
            return pltpu.make_async_remote_copy(
                src_ref=block, dst_ref=block, send_sem=ss.at[i], recv_sem=rs.at[i],
                device_id=target, device_id_type=MESH,
            )

        def start(block):
            descriptor(block).start()

        total = descriptor(whole)
        sent.append(total)
        return start, total

    def received(copies):
        for copy in copies:
            copy.wait_recv()

    def load(i, src, dst):
        copy = pltpu.make_async_copy(src, dst, local_sems.at[i])
        copy.start()
        return copy

    barrier = pltpu.get_barrier_semaphore()
    partners = [on_core()] + [on_xc(k, flip) for k in (1, 2, 3) for flip in (False, True)]
    partners += [on_y(k) for k in range(1, 8)] + [on_z(k) for k in range(1, 8)]
    for target in partners:
        pl.semaphore_signal(barrier, inc=1, device_id=target, device_id_type=MESH)

    load_resid = load(9, resid_hbm, resid_ref)
    load_decb = load(0, decb_hbm, decb.at[0])
    load_orig = load(1, orig_hbm, orig)
    load_enc = load(2, enc_hbm, enc)
    load_encb = load(3, encb_hbm, encb.at[0])
    load_dec = load(4, dec_hbm, dec)
    load_gain = load(5, gain_hbm, gain_ref.at[0])
    load_unemb = load(6, unemb_hbm, unemb)

    piece = x * 2 + core
    load_decb.wait()
    load_resid.wait()
    cols = pl.ds(pl.multiple_of(jnp.minimum(piece, 6) * 512, 512), 512)
    mine = resid_ref[:, cols].astype(F32) - decb[:, cols]
    zx[zlo, 0:4, :] = mine[:, 0:256]
    zx[zlo, 4:8, :] = mine[:, 256:512]
    for r in range(2):
        acc[r, :, HALF:2048] = jnp.zeros((16, 256), F32)
        zs[r, :, HALF:2048] = jnp.zeros((16, 256), BF16)
        zs2[r, :, HALF:2048] = jnp.zeros((16, 256), BF16)
    pl.semaphore_wait(barrier, len(partners))

    copies = [send(zx.at[zlo], zx.at[zlo], on_z(k)) for k in (2, 1, 7)]
    row = lax.broadcasted_iota(jnp.int32, (ROWS, ROWS), 0)
    col = lax.broadcasted_iota(jnp.int32, (ROWS, ROWS), 1)

    def natural(i):
        return ((i >> 2) & 3) * 32 + (i >> 4) * 4 + (i & 3)

    load_orig.wait()
    o = dot(jnp.where(col == natural(row), 1.0, 0.0).astype(BF16), orig[...])
    olog[...] = o
    eo[...] = jnp.exp(o)
    received(copies)
    for k in range(4):
        xf[4 * k : 4 * k + 4, 0:256] = zx[k, 0:4, :]
        xf[4 * k : 4 * k + 4, 256:512] = zx[k, 4:8, :]
    cols_q = block_of(piece, 512)
    rows_y = block_of(y, 16)
    xi[rows_y, cols_q] = xf[...].astype(BF16)
    block = xi.at[rows_y, cols_q]
    copies = {k: send(block, block, on_y(k)) for k in (4, 3, 5, 2, 6, 1, 7)}
    block = xi.at[:, cols_q]
    pieces = [group(on_x(k), block) for k in (1, 2, 3)]

    def forward_rows(k):
        here = xi.at[block_of(lax.rem(y - k + 8, 8), 16), cols_q]
        for start, _ in pieces:
            start(here)

    forward_rows(0)
    for k in (1, 7, 2, 6, 3, 5, 4):
        copies[k].wait_recv()
        forward_rows(k)
    forwards = [send(block, block, on_core())]
    for k in (1, 3, 2):
        pieces[k - 1][1].wait_recv()
        q = lax.rem(x - k + 4, 4) * 2 + core
        block = xi.at[:, block_of(q, 512)]
        forwards.append(send(block, block, on_core()))
    load_enc.wait()
    load_encb.wait()
    received(forwards)

    pre = encb[...]
    for j in range(7):
        cols = pl.ds(j * 512, 512)
        pre = pre + dot(xi[:, cols], enc[:, cols], NT)
    four = 4.0 * pre
    acts = (jnp.maximum(four, 0.0) + jnp.log1p(jnp.exp(-jnp.abs(four)))) * 0.25
    acts_ref[...] = acts.astype(BF16)
    sig[...] = jax.nn.sigmoid(four)
    load_dec.wait()

    cols_z = block_of(z, 256)

    def all_reduce(r, left, right, core_out, core_in, xs, xr, zs, zr, ye, full, bias):
        def term(half, j):
            return dot(left, right[:, pl.ds(pl.multiple_of(half * HALF + j * 256, 256), 256)])

        copies = []
        for begin, end in ((0, 4), (4, 7)):
            for j in range(begin, end):
                core_out[r, :, pl.ds(j * 256, 256)] = term(other, j).astype(BF16)
            cols = pl.ds(begin * 256, (end - begin) * 256)
            copies.append(send(core_out.at[r, :, cols], core_in.at[r, :, cols], on_core()))
        for j in range(7):
            p_own[r, :, pl.ds(j * 256, 256)] = term(core, j)
        yield
        received(copies)
        for j in range(7):
            cols = pl.ds(j * 256, 256)
            s = p_own[r, :, cols] + core_in[r, :, cols].astype(F32)
            p_own[r, :, cols] = s
            xs[r, :, cols] = s.astype(BF16)
        copies = []
        for k in (2, 1, 3):
            there = block_of(lax.rem(x + k, 4), 16)
            copies.append(send(xs.at[r, there, :], xr.at[r, k - 1], on_x(k)))
        yield
        received(copies)
        s = p_own[r, block_of(x, 16), :]
        for k in range(3):
            s = s + xr[r, k].astype(F32)
        acc[r, :, 0:HALF] = s
        zs[r, :, 0:HALF] = s.astype(BF16)
        copies = []
        for k in (4, 3, 5, 2, 6, 1, 7):
            there = block_of(lax.rem(z + k, 8), 256)
            copies.append(send(zs.at[r, :, there], zr.at[r, k - 1], on_z(k)))
        yield
        received(copies)
        s = acc[r, :, cols_z]
        for k in range(7):
            s = s + zr[r, k].astype(F32)
        ye[r, y] = s.astype(BF16)
        copies = [send(ye.at[r, y], ye.at[r, y], on_y(k)) for k in (4, 3, 5, 2, 6, 1, 7)]
        yield
        received(copies)
        s = ye[r, 0].astype(F32)
        for k in range(1, 8):
            s = s + ye[r, k].astype(F32)
        if bias is not None:
            begin = pl.multiple_of(core * HALF + jnp.minimum(z, 6) * 256, 256)
            s = s + bias[:, pl.ds(begin, 256)]
        rows_x = block_of(4 * r + x, 16)
        full[core, rows_x, cols_z] = s.astype(BF16)
        block = full.at[core, rows_x, cols_z]
        copies = {k: send(block, block, on_z(k)) for k in (4, 3, 5, 2, 6, 1, 7)}
        whole = full.at[core, rows_x, :]
        pieces = [group(on_x(k), whole) for k in (1, 2, 3)]

        def forward_columns(k):
            here = full.at[core, rows_x, block_of(lax.rem(z - k + 8, 8), 256)]
            for start, _ in pieces:
                start(here)

        forward_columns(0)
        yield
        for first, second in ((1, 7), (2, 6)):
            copies[first].wait_recv()
            forward_columns(first)
            copies[second].wait_recv()
            forward_columns(second)
        yield
        for k in (3, 5, 4):
            copies[k].wait_recv()
            forward_columns(k)
        block = full.at[core, rows_x, pl.ds(0, HALF)]
        forwards = [send(block, block, on_core())]
        yield
        for k in (1, 3, 2):
            pieces[k - 1][1].wait_recv()
            here = block_of(4 * r + lax.rem(x - k + 4, 4), 16)
            block = full.at[core, here, pl.ds(0, HALF)]
            forwards.append(send(block, block, on_core()))
        yield
        received(forwards)

    def exchange(buffer, value, here, count, target):
        buffer[here] = value
        order = [k for k in (4, 3, 5, 2, 6, 1, 7) if k < count]
        copies = [send(buffer.at[here], buffer.at[here], target(k)) for k in order]
        yield
        received(copies)
        total = buffer[0]
        for k in range(1, count):
            total = total + buffer[k]
        return total

    kls = [None, None]
    dpres = [None, None]

    def chain(r):
        rows = pl.ds(r * CHAIN, CHAIN)
        yield from all_reduce(
            r, acts_ref[rows, :], dec, core_out, core_in, xs, xr, zs, zr, ye, xh, decb
        )
        squares = jnp.zeros((CHAIN, 256), F32)
        for half in range(2):
            for j in range(7):
                v = xh[half, rows, pl.ds(j * 256, 256)].astype(F32)
                squares = squares + v * v
        rinv = lax.rsqrt(jnp.sum(squares, axis=1, keepdims=True) * (1.0 / D) + 1e-06)
        if r == 0:
            load_gain.wait()
            load_unemb.wait()
        raw = jnp.zeros((CHAIN, VOC), F32)
        for half in range(2):
            for j in range(7):
                cols = pl.ds(half * HALF + j * 256, 256)
                v = xh[half, rows, pl.ds(j * 256, 256)].astype(F32)
                normed = (v * rinv * gain_ref[:, cols]).astype(BF16)
                raw = raw + dot(normed, unemb[:, cols], NT)
        shape = jnp.tanh(raw * (1.0 / 30.0))
        capped = 30.0 * shape
        exp_model = jnp.exp(capped)
        exp_orig = eo[rows, :]

        lane = lax.broadcasted_iota(jnp.int32, (CHAIN, ROWS), 1)
        sums = jnp.where(lane == 0, jnp.sum(exp_model, axis=1, keepdims=True), 0.0)
        sums = jnp.where(lane == 1, jnp.sum(exp_orig, axis=1, keepdims=True), sums)
        cross = jnp.sum(exp_orig * (olog[rows, :] - capped), axis=1, keepdims=True)
        sums = jnp.where(lane == 2, cross, sums)
        s = jnp.concatenate([sums, jnp.zeros((CHAIN, ROWS), F32)], axis=0).T[0:4, :]
        here = x * 2 + core
        slot = small_x.at[r, here]
        slot[...] = s
        copies = [send(slot, slot, on_xc(k, f)) for k in (2, 1, 3, 0) for f in (True, False) if k or f]
        yield
        received(copies)
        s = small_x[r, 0]
        for k in range(1, 8):
            s = s + small_x[r, k]
        s = yield from exchange(small_z.at[r], s, z, 8, on_z)
        s = yield from exchange(small_y.at[r], s, y, 8, on_y)
        kls[r] = s[2:3] / s[1:2] - jnp.log(s[1:2]) + jnp.log(s[0:1])
        columns = jnp.concatenate([s, jnp.zeros((ROWS - 4, ROWS), F32)], axis=0).T[0:CHAIN, :]
        dcap = exp_model * (1.0 / columns[:, 0:1]) - exp_orig * (1.0 / columns[:, 1:2])
        dz = (dcap * (1.0 - shape * shape)).astype(BF16)
        yield from all_reduce(
            r, dz, unemb, core_out2, core_in2, xs2, xr2, zs2, zr2, ye2, dn, None
        )
        dots = jnp.zeros((CHAIN, 256), F32)
        for half in range(2):
            for j in range(7):
                cols = pl.ds(j * 256, 256)
                gain = gain_ref[:, pl.ds(half * HALF + j * 256, 256)]
                dots = dots + xh[half, rows, cols].astype(F32) * (dn[half, rows, cols].astype(F32) * gain)
        factor = jnp.sum(dots, axis=1, keepdims=True) * (1.0 / D) * rinv * rinv
        back = jnp.zeros((CHAIN, LAT), F32)
        for half in range(2):
            for j in range(7):
                cols = pl.ds(j * 256, 256)
                whole = pl.ds(half * HALF + j * 256, 256)
                scaled = dn[half, rows, cols].astype(F32) * gain_ref[:, whole]
                dxhat = rinv * (scaled - xh[half, rows, cols].astype(F32) * factor)
                brow[r, :, whole] = jnp.sum(dxhat, axis=0, keepdims=True)
                rounded = dxhat.astype(BF16)
                dxl[rows, whole] = rounded
                back = back + dot(rounded, dec[:, whole], NT)
        dpres[r] = back * sig[rows, :]

    running = [chain(0), chain(1)]
    while running:
        for generator in list(running):
            try:
                next(generator)
            except StopIteration:
                running.remove(generator)

    dpre = jnp.concatenate(dpres, axis=0)
    ebg = jnp.sum(dpre, axis=0, keepdims=True)
    ebg_ref[...] = ebg

    high = ebg.astype(BF16).astype(F32)
    middle = (ebg - high).astype(BF16).astype(F32)
    last = ebg - high - middle
    stacked = jnp.concatenate([high, middle, last, jnp.zeros((13, LAT), F32)], axis=0).astype(BF16)
    for j in range(7):
        part = dot(stacked, enc[:, 512 * j : 512 * j + 512])
        th[j : j + 1, :] = part[0:1] + part[1:2] + part[2:3]
    th[7:8, :] = jnp.zeros((1, 512), F32)
    here, there = block_of(core, 256), block_of(other, 256)
    copy = send(th.at[:, there], th_c, on_core())
    acts_t = acts_ref[...].astype(F32).T.astype(BF16)
    dpre_t = dpre.T.astype(BF16)
    copy.wait_recv()

    stores = []
    n_sent = len(sent)

    def row_kl():
        rest = jnp.zeros((8, ROWS), F32)
        for r in range(2):
            perm = jnp.where((col == natural(row + CHAIN * r)) & (row < CHAIN), 1.0, 0.0)
            kl = jnp.where(lax.broadcasted_iota(jnp.int32, (8, ROWS), 1) < CHAIN, kls[r], 0.0)
            rest = rest + dot(kl, perm, precision=lax.Precision.HIGHEST)
        kl_ref[...] = rest
        stores.append(load(10, kl_ref.at[0], kl_hbm))
        stores.append(load(11, ebg_ref.at[0], ebg_hbm))

    def grad_dec():
        for j in range(7):
            cols = pl.ds(j * 512, 512)
            gdec[:, cols] = dot(acts_t, dxl[:, cols]).astype(BF16)
        stores.append(load(7, gdec, gdec_hbm))

    def grad_enc():
        for j in range(7):
            cols = pl.ds(j * 512, 512)
            genc[:, cols] = dot(dpre_t, xi[:, cols]).astype(BF16)
        stores.append(load(8, genc, genc_hbm))
        for copy in sent[:n_sent]:
            copy.wait_send()

    total = yield_through(exchange(th_x, th[:, here] + th_c[...], x, 4, on_x), row_kl)
    total = yield_through(exchange(th_z, total, z, 8, on_z), grad_dec)
    total = yield_through(exchange(th_y, total, y, 8, on_y), grad_enc)
    th_all[:, here] = total
    copy = send(th_all.at[:, here], th_all.at[:, here], on_core())
    copy.wait_recv()
    for j in range(7):
        cols = pl.ds(512 * j, 512)
        gbd_ref[:, cols] = brow[0, :, cols] + brow[1, :, cols] - th_all[j : j + 1, :]
    stores.append(load(12, gbd_ref.at[0], gbd_hbm))
    for copy in sent[n_sent:]:
        copy.wait_send()
    for store in stores:
        store.wait()


def yield_through(generator, meanwhile):
    next(generator)
    meanwhile()
    try:
        next(generator)
    except StopIteration as end:
        return end.value


def copy_out(*refs):
    ins, outs, held, sems = refs[0:5], refs[5:10], refs[10:15], refs[15]

    def views(refs):
        return [ref.at[0] if len(ref.shape) == 2 and ref.shape[0] == 1 else ref for ref in refs]

    held = views(held)
    loads = [pltpu.make_async_copy(ins[i], held[i], sems.at[0, i]) for i in range(5)]
    stores = [pltpu.make_async_copy(held[i], outs[i], sems.at[1, i]) for i in range(5)]
    for copy in loads:
        copy.start()
    for load, store in zip(loads, stores):
        load.wait()
        store.start()
    for copy in stores:
        copy.wait()


def per_device(resid, enc_weight, enc_bias, dec_weight, dec_bias, norm_gain, unembed, orig_logits):
    hbm = pl.BlockSpec(memory_space=pl.ANY)
    reduce_scratch = [
        pltpu.VMEM((2, CHAIN, HALF), BF16),
        pltpu.VMEM((2, CHAIN, HALF), BF16),
        pltpu.VMEM((2, CHAIN, HALF), BF16),
        pltpu.VMEM((2, 3, 16, HALF), BF16),
        pltpu.VMEM((2, 16, 2048), BF16),
        pltpu.VMEM((2, 7, 16, 256), BF16),
        pltpu.VMEM((2, 8, 16, 256), BF16),
        pltpu.VMEM((2, ROWS, 2048), BF16),
    ]
    shapes = (
        jax.ShapeDtypeStruct((LAT, D), BF16),
        jax.ShapeDtypeStruct((LAT, D), BF16),
        jax.ShapeDtypeStruct((LAT,), F32),
        jax.ShapeDtypeStruct((D,), F32),
        jax.ShapeDtypeStruct((ROWS,), F32),
    )
    results = pl.pallas_call(
        kernel,
        out_shape=shapes,
        in_specs=[hbm] * 8,
        out_specs=(hbm,) * 5,
        scratch_shapes=[
            pltpu.VMEM((4, D), BF16),
            pltpu.VMEM((1, LAT), F32),
            pltpu.VMEM((1, D), F32),
            pltpu.VMEM((8, ROWS), F32),
            pltpu.VMEM((LAT, D), BF16),
            pltpu.VMEM((LAT, D), BF16),
            pltpu.VMEM((VOC, D), BF16),
            pltpu.VMEM((1, LAT), F32),
            pltpu.VMEM((1, D), F32),
            pltpu.VMEM((1, D), F32),
            pltpu.VMEM((ROWS, VOC), BF16),
            pltpu.VMEM((LAT, D), BF16),
            pltpu.VMEM((LAT, D), BF16),
            pltpu.VMEM((4, 8, 256), F32),
            pltpu.VMEM((16, 512), F32),
            pltpu.VMEM((ROWS, 4096), BF16),
            pltpu.VMEM((2, CHAIN, HALF), F32),
            pltpu.VMEM((2, 16, 2048), F32),
            *reduce_scratch,
            *reduce_scratch,
            pltpu.VMEM((ROWS, VOC), F32),
            pltpu.VMEM((ROWS, VOC), F32),
            pltpu.VMEM((ROWS, LAT), F32),
            pltpu.VMEM((ROWS, LAT), BF16),
            pltpu.VMEM((ROWS, D), BF16),
            pltpu.VMEM((2, 1, D), F32),
            *(pltpu.VMEM((2, 8, 4, ROWS), F32) for _ in range(3)),
            pltpu.VMEM((8, 512), F32),
            pltpu.VMEM((8, 256), F32),
            *(pltpu.VMEM((n, 8, 256), F32) for n in (4, 8, 8)),
            pltpu.VMEM((8, 512), F32),
            pltpu.SemaphoreType.DMA((13,)),
            pltpu.SemaphoreType.DMA((N_SEMS,)),
            pltpu.SemaphoreType.DMA((N_SEMS,)),
        ],
        compiler_params=pltpu.CompilerParams(
            collective_id=0, has_side_effects=True, vmem_limit_bytes=60 * 2**20
        ),
        cost_estimate=pl.CostEstimate(flops=10**9, bytes_accessed=5 * 10**6, transcendentals=0),
        name="train_step",
    )(resid, enc_weight, enc_bias, dec_weight, dec_bias, norm_gain, unembed, orig_logits)
    return pl.pallas_call(
        copy_out,
        out_shape=shapes,
        in_specs=[hbm] * 5,
        out_specs=(hbm,) * 5,
        scratch_shapes=[
            pltpu.VMEM((LAT, D), BF16),
            pltpu.VMEM((LAT, D), BF16),
            pltpu.VMEM((1, LAT), F32),
            pltpu.VMEM((1, D), F32),
            pltpu.VMEM((1, ROWS), F32),
            pltpu.SemaphoreType.DMA((2, 5)),
        ],
        compiler_params=pltpu.CompilerParams(vmem_limit_bytes=60 * 2**20),
        name="copy_out",
    )(*results)


def solution(mesh):
    split = P(("tok", "lat"), None)
    return jax.shard_map(
        per_device,
        mesh=mesh,
        in_specs=(
            P("tok", None), split, P(("tok", "lat")), split, P(), P(), split,
            P(None, ("tok", "lat")),
        ),
        out_specs=(split, split, P(("tok", "lat")), P(), P()),
        check_vma=False,
    )
```

```python
import jax
import jax.numpy as jnp
from jax import lax
from jax.experimental import pallas as pl
from jax.experimental.pallas import tpu as pltpu
from jax.sharding import PartitionSpec as P

MESH = pl.DeviceIdType.MESH
F32, BF16 = jnp.float32, jnp.bfloat16
D, ROWS, LAT, VOC = 3584, 128, 96, 256
HALF = D // 2
CHAIN = ROWS // 2
NN = (((1,), (0,)), ((), ()))
NT = (((1,), (1,)), ((), ()))
N_SEMS = 240


def dot(a, b, dims=NN, precision=None):
    return lax.dot_general(a, b, dims, preferred_element_type=F32, precision=precision)


def block_of(index, size):
    return pl.ds(pl.multiple_of(index * size, size), size)


def kernel(
    resid_hbm, enc_hbm, encb_hbm, dec_hbm, decb_hbm, gain_hbm, unemb_hbm, orig_hbm,
    genc_hbm, gdec_hbm, ebg_hbm, gbd_hbm, kl_hbm,
    resid_ref, ebg_ref, gbd_ref, kl_ref,
    enc, dec, unemb, encb, decb, gain_ref, orig, genc, gdec,
    zx, xf, xi, p_own, acc,
    core_out, core_in, xs, xr, zs, zr, ye, xh,
    core_out2, core_in2, xs2, xr2, zs2, zr2, ye2, dn,
    eo, olog, sig, acts_ref, dxl, brow,
    small_x, small_z, small_y,
    th, th_c, th_x, th_z, th_y, th_all,
    local_sems, ss, rs,
):
    t, l = lax.axis_index("tok"), lax.axis_index("lat")
    zlo, y = lax.div(t, 8), lax.rem(t, 8)
    x, zhi, core = lax.div(l, 4), lax.rem(lax.div(l, 2), 2), lax.rem(l, 2)
    z = zhi * 4 + zlo
    other = 1 - core

    def device(x, y, z, c):
        return (lax.rem(z, 4) * 8 + y, x * 4 + lax.div(z, 4) * 2 + c)

    def on_core():
        return device(x, y, z, other)

    def on_x(k):
        return device(lax.rem(x + k, 4), y, z, core)

    def on_xc(k, flip):
        return device(lax.rem(x + k, 4), y, z, other if flip else core)

    def on_y(k):
        return device(x, lax.rem(y + k, 8), z, core)

    def on_z(k):
        return device(x, y, lax.rem(z + k, 8), core)

    counter = [0]
    sent = []

    def send(src, dst, target):
        i = counter[0]
        counter[0] += 1
        copy = pltpu.make_async_remote_copy(
            src_ref=src, dst_ref=dst, send_sem=ss.at[i], recv_sem=rs.at[i],
            device_id=target, device_id_type=MESH,
        )
        copy.start()
        sent.append(copy)
        return copy

    def group(target, whole):
        i = counter[0]
        counter[0] += 1

        def descriptor(block):
            return pltpu.make_async_remote_copy(
                src_ref=block, dst_ref=block, send_sem=ss.at[i], recv_sem=rs.at[i],
                device_id=target, device_id_type=MESH,
            )

        def start(block):
            descriptor(block).start()

        total = descriptor(whole)
        sent.append(total)
        return start, total

    def received(copies):
        for copy in copies:
            copy.wait_recv()

    def load(i, src, dst):
        copy = pltpu.make_async_copy(src, dst, local_sems.at[i])
        copy.start()
        return copy

    barrier = pltpu.get_barrier_semaphore()
    partners = [on_core()] + [on_xc(k, flip) for k in (1, 2, 3) for flip in (False, True)]
    partners += [on_y(k) for k in range(1, 8)] + [on_z(k) for k in range(1, 8)]
    for target in partners:
        pl.semaphore_signal(barrier, inc=1, device_id=target, device_id_type=MESH)

    load_resid = load(9, resid_hbm, resid_ref)
    load_decb = load(0, decb_hbm, decb.at[0])
    load_orig = load(1, orig_hbm, orig)
    load_enc = load(2, enc_hbm, enc)
    load_encb = load(3, encb_hbm, encb.at[0])
    load_dec = load(4, dec_hbm, dec)
    load_gain = load(5, gain_hbm, gain_ref.at[0])
    load_unemb = load(6, unemb_hbm, unemb)

    piece = x * 2 + core
    load_decb.wait()
    load_resid.wait()
    cols = pl.ds(pl.multiple_of(jnp.minimum(piece, 6) * 512, 512), 512)
    mine = resid_ref[:, cols].astype(F32) - decb[:, cols]
    zx[zlo, 0:4, :] = mine[:, 0:256]
    zx[zlo, 4:8, :] = mine[:, 256:512]
    for r in range(2):
        acc[r, :, HALF:2048] = jnp.zeros((16, 256), F32)
        zs[r, :, HALF:2048] = jnp.zeros((16, 256), BF16)
        zs2[r, :, HALF:2048] = jnp.zeros((16, 256), BF16)
    pl.semaphore_wait(barrier, len(partners))

    copies = [send(zx.at[zlo], zx.at[zlo], on_z(k)) for k in (2, 1, 7)]
    row = lax.broadcasted_iota(jnp.int32, (ROWS, ROWS), 0)
    col = lax.broadcasted_iota(jnp.int32, (ROWS, ROWS), 1)

    def natural(i):
        return ((i >> 2) & 3) * 32 + (i >> 4) * 4 + (i & 3)

    load_orig.wait()
    o = dot(jnp.where(col == natural(row), 1.0, 0.0).astype(BF16), orig[...])
    olog[...] = o
    eo[...] = jnp.exp(o)
    received(copies)
    for k in range(4):
        xf[4 * k : 4 * k + 4, 0:256] = zx[k, 0:4, :]
        xf[4 * k : 4 * k + 4, 256:512] = zx[k, 4:8, :]
    cols_q = block_of(piece, 512)
    rows_y = block_of(y, 16)
    xi[rows_y, cols_q] = xf[...].astype(BF16)
    block = xi.at[rows_y, cols_q]
    copies = {k: send(block, block, on_y(k)) for k in (4, 3, 5, 2, 6, 1, 7)}
    block = xi.at[:, cols_q]
    pieces = [group(on_x(k), block) for k in (1, 2, 3)]

    def forward_rows(k):
        here = xi.at[block_of(lax.rem(y - k + 8, 8), 16), cols_q]
        for start, _ in pieces:
            start(here)

    forward_rows(0)
    for k in (1, 7, 2, 6, 3, 5, 4):
        copies[k].wait_recv()
        forward_rows(k)
    forwards = [send(block, block, on_core())]
    for k in (1, 3, 2):
        pieces[k - 1][1].wait_recv()
        q = lax.rem(x - k + 4, 4) * 2 + core
        block = xi.at[:, block_of(q, 512)]
        forwards.append(send(block, block, on_core()))
    load_enc.wait()
    load_encb.wait()
    received(forwards)

    pre = encb[...]
    for j in range(7):
        cols = pl.ds(j * 512, 512)
        pre = pre + dot(xi[:, cols], enc[:, cols], NT)
    four = 4.0 * pre
    acts = (jnp.maximum(four, 0.0) + jnp.log1p(jnp.exp(-jnp.abs(four)))) * 0.25
    acts_ref[...] = acts.astype(BF16)
    sig[...] = jax.nn.sigmoid(four)
    load_dec.wait()
    load_gain.wait()
    load_unemb.wait()

    cols_z = block_of(z, 256)

    def all_reduce(r, left, right, core_out, core_in, xs, xr, zs, zr, ye, full, bias, early):
        def term(half, j):
            return dot(left, right[:, pl.ds(pl.multiple_of(half * HALF + j * 256, 256), 256)])

        copies = []
        for begin, end in ((0, 4), (4, 7)):
            for j in range(begin, end):
                core_out[r, :, pl.ds(j * 256, 256)] = term(other, j).astype(BF16)
            cols = pl.ds(begin * 256, (end - begin) * 256)
            copies.append(send(core_out.at[r, :, cols], core_in.at[r, :, cols], on_core()))
        yield
        out = []
        for (begin, end), copy in zip(((0, 4), (4, 7)), copies):
            copy.wait_recv()
            for j in range(begin, end):
                cols = pl.ds(j * 256, 256)
                s = term(core, j) + core_in[r, :, cols].astype(F32)
                p_own[r, :, cols] = s
                xs[r, :, cols] = s.astype(BF16)
            cols = pl.ds(begin * 256, (end - begin) * 256)
            for k in (2, 1, 3):
                there = block_of(lax.rem(x + k, 4), 16)
                out.append(send(xs.at[r, there, cols], xr.at[r, k - 1, :, cols], on_x(k)))
        copies = out
        yield
        received(copies)
        s = p_own[r, block_of(x, 16), :]
        for k in range(3):
            s = s + xr[r, k].astype(F32)
        acc[r, :, 0:HALF] = s
        zs[r, :, 0:HALF] = s.astype(BF16)
        copies = []
        for k in (4, 3, 5, 2, 6, 1, 7):
            there = block_of(lax.rem(z + k, 8), 256)
            copies.append(send(zs.at[r, :, there], zr.at[r, k - 1], on_z(k)))
        yield
        received(copies)
        s = acc[r, :, cols_z]
        for k in range(7):
            s = s + zr[r, k].astype(F32)
        ye[r, y] = s.astype(BF16)
        copies = [send(ye.at[r, y], ye.at[r, y], on_y(k)) for k in (4, 3, 5, 2, 6, 1, 7)]
        yield
        received(copies)
        s = ye[r, 0].astype(F32)
        for k in range(1, 8):
            s = s + ye[r, k].astype(F32)
        if bias is not None:
            begin = pl.multiple_of(core * HALF + jnp.minimum(z, 6) * 256, 256)
            s = s + bias[:, pl.ds(begin, 256)]
        rows_x = block_of(4 * r + x, 16)
        full[core, rows_x, cols_z] = s.astype(BF16)
        block = full.at[core, rows_x, cols_z]
        copies = {k: send(block, block, on_z(k)) for k in (4, 3, 5, 2, 6, 1, 7)}
        whole = full.at[core, rows_x, :]
        pieces = [group(on_x(k), whole) for k in (1, 2, 3)]

        def forward_columns(k):
            here = full.at[core, rows_x, block_of(lax.rem(z - k + 8, 8), 256)]
            for start, _ in pieces:
                start(here)

        forward_columns(0)
        yield
        for first, second in ((1, 7), (2, 6)):
            copies[first].wait_recv()
            forward_columns(first)
            copies[second].wait_recv()
            forward_columns(second)
        yield
        for k in (3, 5, 4):
            copies[k].wait_recv()
            forward_columns(k)
        block = full.at[core, rows_x, pl.ds(0, HALF)]
        forwards = [send(block, block, on_core())]
        yield
        for k in (1, 3, 2):
            pieces[k - 1][1].wait_recv()
            here = block_of(4 * r + lax.rem(x - k + 4, 4), 16)
            block = full.at[core, here, pl.ds(0, HALF)]
            forwards.append(send(block, block, on_core()))
        early()
        yield
        received(forwards)

    def exchange(buffer, value, here, count, target):
        buffer[here] = value
        order = [k for k in (4, 3, 5, 2, 6, 1, 7) if k < count]
        copies = [send(buffer.at[here], buffer.at[here], target(k)) for k in order]
        yield
        received(copies)
        total = buffer[0]
        for k in range(1, count):
            total = total + buffer[k]
        return total

    kls = [None, None]
    dpres = [None, None]

    def chain(r):
        rows = pl.ds(r * CHAIN, CHAIN)
        squares = [jnp.zeros((CHAIN, 256), F32)]
        raw = [jnp.zeros((CHAIN, VOC), F32)]

        def logit_terms(half):
            for j in range(7):
                cols = pl.ds(pl.multiple_of(half * HALF + j * 256, 256), 256)
                v = xh[half, rows, pl.ds(j * 256, 256)].astype(F32)
                squares[0] = squares[0] + v * v
                raw[0] = raw[0] + dot((v * gain_ref[:, cols]).astype(BF16), unemb[:, cols], NT)

        yield from all_reduce(
            r, acts_ref[rows, :], dec, core_out, core_in, xs, xr, zs, zr, ye, xh, decb,
            lambda: logit_terms(core),
        )
        logit_terms(other)
        rinv = lax.rsqrt(jnp.sum(squares[0], axis=1, keepdims=True) * (1.0 / D) + 1e-06)
        raw = raw[0] * rinv
        shape = jnp.tanh(raw * (1.0 / 30.0))
        capped = 30.0 * shape
        exp_model = jnp.exp(capped)
        exp_orig = eo[rows, :]

        lane = lax.broadcasted_iota(jnp.int32, (CHAIN, ROWS), 1)
        sums = jnp.where(lane == 0, jnp.sum(exp_model, axis=1, keepdims=True), 0.0)
        sums = jnp.where(lane == 1, jnp.sum(exp_orig, axis=1, keepdims=True), sums)
        cross = jnp.sum(exp_orig * (olog[rows, :] - capped), axis=1, keepdims=True)
        sums = jnp.where(lane == 2, cross, sums)
        s = jnp.concatenate([sums, jnp.zeros((CHAIN, ROWS), F32)], axis=0).T[0:4, :]
        here = x * 2 + core
        slot = small_x.at[r, here]
        slot[...] = s
        copies = [send(slot, slot, on_xc(k, f)) for k in (2, 1, 3, 0) for f in (True, False) if k or f]
        yield
        received(copies)
        s = small_x[r, 0]
        for k in range(1, 8):
            s = s + small_x[r, k]
        s = yield from exchange(small_z.at[r], s, z, 8, on_z)
        s = yield from exchange(small_y.at[r], s, y, 8, on_y)
        kls[r] = s[2:3] / s[1:2] - jnp.log(s[1:2]) + jnp.log(s[0:1])
        columns = jnp.concatenate([s, jnp.zeros((ROWS - 4, ROWS), F32)], axis=0).T[0:CHAIN, :]
        dcap = exp_model * (1.0 / columns[:, 0:1]) - exp_orig * (1.0 / columns[:, 1:2])
        dz = (dcap * (1.0 - shape * shape)).astype(BF16)
        dots = [jnp.zeros((CHAIN, 256), F32)]

        def dot_terms(half):
            for j in range(7):
                cols = pl.ds(j * 256, 256)
                gain = gain_ref[:, pl.ds(pl.multiple_of(half * HALF + j * 256, 256), 256)]
                scaled = dn[half, rows, cols].astype(F32) * gain
                dots[0] = dots[0] + xh[half, rows, cols].astype(F32) * scaled

        yield from all_reduce(
            r, dz, unemb, core_out2, core_in2, xs2, xr2, zs2, zr2, ye2, dn, None,
            lambda: dot_terms(core),
        )
        dot_terms(other)
        factor = jnp.sum(dots[0], axis=1, keepdims=True) * (1.0 / D) * rinv * rinv
        back = jnp.zeros((CHAIN, LAT), F32)
        for half in range(2):
            for j in range(7):
                cols = pl.ds(j * 256, 256)
                whole = pl.ds(half * HALF + j * 256, 256)
                scaled = dn[half, rows, cols].astype(F32) * gain_ref[:, whole]
                dxhat = rinv * (scaled - xh[half, rows, cols].astype(F32) * factor)
                brow[r, :, whole] = jnp.sum(dxhat, axis=0, keepdims=True)
                rounded = dxhat.astype(BF16)
                dxl[rows, whole] = rounded
                back = back + dot(rounded, dec[:, whole], NT)
        dpres[r] = back * sig[rows, :]

    running = [chain(0), chain(1)]
    while running:
        for generator in list(running):
            try:
                next(generator)
            except StopIteration:
                running.remove(generator)

    dpre = jnp.concatenate(dpres, axis=0)
    ebg = jnp.sum(dpre, axis=0, keepdims=True)
    ebg_ref[...] = ebg

    high = ebg.astype(BF16).astype(F32)
    middle = (ebg - high).astype(BF16).astype(F32)
    last = ebg - high - middle
    stacked = jnp.concatenate([high, middle, last, jnp.zeros((13, LAT), F32)], axis=0).astype(BF16)
    for j in range(7):
        part = dot(stacked, enc[:, 512 * j : 512 * j + 512])
        th[j : j + 1, :] = part[0:1] + part[1:2] + part[2:3]
    th[7:8, :] = jnp.zeros((1, 512), F32)
    here, there = block_of(core, 256), block_of(other, 256)
    copy = send(th.at[:, there], th_c, on_core())
    acts_t = acts_ref[...].astype(F32).T.astype(BF16)
    dpre_t = dpre.T.astype(BF16)
    copy.wait_recv()

    stores = []
    n_sent = len(sent)

    def row_kl():
        rest = jnp.zeros((8, ROWS), F32)
        for r in range(2):
            perm = jnp.where((col == natural(row + CHAIN * r)) & (row < CHAIN), 1.0, 0.0)
            kl = jnp.where(lax.broadcasted_iota(jnp.int32, (8, ROWS), 1) < CHAIN, kls[r], 0.0)
            rest = rest + dot(kl, perm, precision=lax.Precision.HIGHEST)
        kl_ref[...] = rest
        stores.append(load(10, kl_ref.at[0], kl_hbm))
        stores.append(load(11, ebg_ref.at[0], ebg_hbm))

    def grad_dec():
        for j in range(7):
            cols = pl.ds(j * 512, 512)
            gdec[:, cols] = dot(acts_t, dxl[:, cols]).astype(BF16)
        stores.append(load(7, gdec, gdec_hbm))

    def grad_enc():
        for j in range(7):
            cols = pl.ds(j * 512, 512)
            genc[:, cols] = dot(dpre_t, xi[:, cols]).astype(BF16)
        stores.append(load(8, genc, genc_hbm))
        for copy in sent[:n_sent]:
            copy.wait_send()

    total = yield_through(exchange(th_x, th[:, here] + th_c[...], x, 4, on_x), row_kl)
    total = yield_through(exchange(th_z, total, z, 8, on_z), grad_dec)
    total = yield_through(exchange(th_y, total, y, 8, on_y), grad_enc)
    th_all[:, here] = total
    copy = send(th_all.at[:, here], th_all.at[:, here], on_core())
    copy.wait_recv()
    for j in range(7):
        cols = pl.ds(512 * j, 512)
        gbd_ref[:, cols] = brow[0, :, cols] + brow[1, :, cols] - th_all[j : j + 1, :]
    stores.append(load(12, gbd_ref.at[0], gbd_hbm))
    for copy in sent[n_sent:]:
        copy.wait_send()
    for store in stores:
        store.wait()


def yield_through(generator, meanwhile):
    next(generator)
    meanwhile()
    try:
        next(generator)
    except StopIteration as end:
        return end.value


def copy_out(*refs):
    ins, outs, held, sems = refs[0:5], refs[5:10], refs[10:15], refs[15]

    def views(refs):
        return [ref.at[0] if len(ref.shape) == 2 and ref.shape[0] == 1 else ref for ref in refs]

    held = views(held)
    loads = [pltpu.make_async_copy(ins[i], held[i], sems.at[0, i]) for i in range(5)]
    stores = [pltpu.make_async_copy(held[i], outs[i], sems.at[1, i]) for i in range(5)]
    for copy in loads:
        copy.start()
    for load, store in zip(loads, stores):
        load.wait()
        store.start()
    for copy in stores:
        copy.wait()


def per_device(resid, enc_weight, enc_bias, dec_weight, dec_bias, norm_gain, unembed, orig_logits):
    hbm = pl.BlockSpec(memory_space=pl.ANY)
    reduce_scratch = [
        pltpu.VMEM((2, CHAIN, HALF), BF16),
        pltpu.VMEM((2, CHAIN, HALF), BF16),
        pltpu.VMEM((2, CHAIN, HALF), BF16),
        pltpu.VMEM((2, 3, 16, HALF), BF16),
        pltpu.VMEM((2, 16, 2048), BF16),
        pltpu.VMEM((2, 7, 16, 256), BF16),
        pltpu.VMEM((2, 8, 16, 256), BF16),
        pltpu.VMEM((2, ROWS, 2048), BF16),
    ]
    shapes = (
        jax.ShapeDtypeStruct((LAT, D), BF16),
        jax.ShapeDtypeStruct((LAT, D), BF16),
        jax.ShapeDtypeStruct((LAT,), F32),
        jax.ShapeDtypeStruct((D,), F32),
        jax.ShapeDtypeStruct((ROWS,), F32),
    )
    results = pl.pallas_call(
        kernel,
        out_shape=shapes,
        in_specs=[hbm] * 8,
        out_specs=(hbm,) * 5,
        scratch_shapes=[
            pltpu.VMEM((4, D), BF16),
            pltpu.VMEM((1, LAT), F32),
            pltpu.VMEM((1, D), F32),
            pltpu.VMEM((8, ROWS), F32),
            pltpu.VMEM((LAT, D), BF16),
            pltpu.VMEM((LAT, D), BF16),
            pltpu.VMEM((VOC, D), BF16),
            pltpu.VMEM((1, LAT), F32),
            pltpu.VMEM((1, D), F32),
            pltpu.VMEM((1, D), F32),
            pltpu.VMEM((ROWS, VOC), BF16),
            pltpu.VMEM((LAT, D), BF16),
            pltpu.VMEM((LAT, D), BF16),
            pltpu.VMEM((4, 8, 256), F32),
            pltpu.VMEM((16, 512), F32),
            pltpu.VMEM((ROWS, 4096), BF16),
            pltpu.VMEM((2, CHAIN, HALF), F32),
            pltpu.VMEM((2, 16, 2048), F32),
            *reduce_scratch,
            *reduce_scratch,
            pltpu.VMEM((ROWS, VOC), F32),
            pltpu.VMEM((ROWS, VOC), F32),
            pltpu.VMEM((ROWS, LAT), F32),
            pltpu.VMEM((ROWS, LAT), BF16),
            pltpu.VMEM((ROWS, D), BF16),
            pltpu.VMEM((2, 1, D), F32),
            *(pltpu.VMEM((2, 8, 4, ROWS), F32) for _ in range(3)),
            pltpu.VMEM((8, 512), F32),
            pltpu.VMEM((8, 256), F32),
            *(pltpu.VMEM((n, 8, 256), F32) for n in (4, 8, 8)),
            pltpu.VMEM((8, 512), F32),
            pltpu.SemaphoreType.DMA((13,)),
            pltpu.SemaphoreType.DMA((N_SEMS,)),
            pltpu.SemaphoreType.DMA((N_SEMS,)),
        ],
        compiler_params=pltpu.CompilerParams(
            collective_id=0, has_side_effects=True, vmem_limit_bytes=60 * 2**20
        ),
        cost_estimate=pl.CostEstimate(flops=10**9, bytes_accessed=5 * 10**6, transcendentals=0),
        name="train_step",
    )(resid, enc_weight, enc_bias, dec_weight, dec_bias, norm_gain, unembed, orig_logits)
    return pl.pallas_call(
        copy_out,
        out_shape=shapes,
        in_specs=[hbm] * 5,
        out_specs=(hbm,) * 5,
        scratch_shapes=[
            pltpu.VMEM((LAT, D), BF16),
            pltpu.VMEM((LAT, D), BF16),
            pltpu.VMEM((1, LAT), F32),
            pltpu.VMEM((1, D), F32),
            pltpu.VMEM((1, ROWS), F32),
            pltpu.SemaphoreType.DMA((2, 5)),
        ],
        compiler_params=pltpu.CompilerParams(vmem_limit_bytes=60 * 2**20),
        name="copy_out",
    )(*results)


def solution(mesh):
    split = P(("tok", "lat"), None)
    return jax.shard_map(
        per_device,
        mesh=mesh,
        in_specs=(
            P("tok", None), split, P(("tok", "lat")), split, P(), P(), split,
            P(None, ("tok", "lat")),
        ),
        out_specs=(split, split, P(("tok", "lat")), P(), P()),
        check_vma=False,
    )
```

```python
import jax
import jax.numpy as jnp
from jax import lax
from jax.experimental import pallas as pl
from jax.experimental.pallas import tpu as pltpu
from jax.sharding import PartitionSpec as P

MESH = pl.DeviceIdType.MESH
F32, BF16 = jnp.float32, jnp.bfloat16
D, ROWS, LAT, VOC = 3584, 128, 96, 256
HALF = D // 2
CHAIN = ROWS // 2
NN = (((1,), (0,)), ((), ()))
NT = (((1,), (1,)), ((), ()))
N_SEMS = 240


def dot(a, b, dims=NN, precision=None):
    return lax.dot_general(a, b, dims, preferred_element_type=F32, precision=precision)


def block_of(index, size):
    return pl.ds(pl.multiple_of(index * size, size), size)


def kernel(
    resid_hbm, enc_hbm, encb_hbm, dec_hbm, decb_hbm, gain_hbm, unemb_hbm, orig_hbm,
    genc_hbm, gdec_hbm, ebg_hbm, gbd_hbm, kl_hbm,
    resid_ref, ebg_ref, gbd_ref, kl_ref,
    enc, dec, unemb, encb, decb, gain_ref, orig, genc, gdec,
    zx, xf, xi, p_own, acc,
    core_out, core_in, xs, xr, zs, zr, ye, xh,
    core_out2, core_in2, xs2, xr2, zs2, zr2, ye2, dn,
    eo, olog, sig, acts_ref, dxl, brow,
    small_x, small_z, small_y,
    th, th_c, th_x, th_z, th_y, th_all,
    local_sems, ss, rs,
):
    t, l = lax.axis_index("tok"), lax.axis_index("lat")
    zlo, y = lax.div(t, 8), lax.rem(t, 8)
    x, zhi, core = lax.div(l, 4), lax.rem(lax.div(l, 2), 2), lax.rem(l, 2)
    z = zhi * 4 + zlo
    other = 1 - core

    def device(x, y, z, c):
        return (lax.rem(z, 4) * 8 + y, x * 4 + lax.div(z, 4) * 2 + c)

    def on_core():
        return device(x, y, z, other)

    def on_x(k):
        return device(lax.rem(x + k, 4), y, z, core)

    def on_xc(k, flip):
        return device(lax.rem(x + k, 4), y, z, other if flip else core)

    def on_y(k):
        return device(x, lax.rem(y + k, 8), z, core)

    def on_z(k):
        return device(x, y, lax.rem(z + k, 8), core)

    counter = [0]
    sent = []

    def send(src, dst, target):
        i = counter[0]
        counter[0] += 1
        copy = pltpu.make_async_remote_copy(
            src_ref=src, dst_ref=dst, send_sem=ss.at[i], recv_sem=rs.at[i],
            device_id=target, device_id_type=MESH,
        )
        copy.start()
        sent.append(copy)
        return copy

    def group(target, whole):
        i = counter[0]
        counter[0] += 1

        def descriptor(block):
            return pltpu.make_async_remote_copy(
                src_ref=block, dst_ref=block, send_sem=ss.at[i], recv_sem=rs.at[i],
                device_id=target, device_id_type=MESH,
            )

        def start(block):
            descriptor(block).start()

        total = descriptor(whole)
        sent.append(total)
        return start, total

    def received(copies):
        for copy in copies:
            copy.wait_recv()

    def load(i, src, dst):
        copy = pltpu.make_async_copy(src, dst, local_sems.at[i])
        copy.start()
        return copy

    barrier = pltpu.get_barrier_semaphore()
    partners = [on_core()] + [on_xc(k, flip) for k in (1, 2, 3) for flip in (False, True)]
    partners += [on_y(k) for k in range(1, 8)] + [on_z(k) for k in range(1, 8)]
    for target in partners:
        pl.semaphore_signal(barrier, inc=1, device_id=target, device_id_type=MESH)

    load_resid = load(9, resid_hbm, resid_ref)
    load_decb = load(0, decb_hbm, decb.at[0])
    load_orig = load(1, orig_hbm, orig)
    load_enc = load(2, enc_hbm, enc)
    load_encb = load(3, encb_hbm, encb.at[0])
    load_dec = load(4, dec_hbm, dec)
    load_gain = load(5, gain_hbm, gain_ref.at[0])
    load_unemb = load(6, unemb_hbm, unemb)

    piece = x * 2 + core
    load_decb.wait()
    load_resid.wait()
    cols = pl.ds(pl.multiple_of(jnp.minimum(piece, 6) * 512, 512), 512)
    mine = resid_ref[:, cols].astype(F32) - decb[:, cols]
    zx[zlo, 0:4, :] = mine[:, 0:256]
    zx[zlo, 4:8, :] = mine[:, 256:512]
    for r in range(2):
        acc[r, :, HALF:2048] = jnp.zeros((16, 256), F32)
        zs[r, :, HALF:2048] = jnp.zeros((16, 256), BF16)
        zs2[r, :, HALF:2048] = jnp.zeros((16, 256), BF16)
    pl.semaphore_wait(barrier, len(partners))

    copies = [send(zx.at[zlo], zx.at[zlo], on_z(k)) for k in (2, 1, 7)]
    row = lax.broadcasted_iota(jnp.int32, (ROWS, ROWS), 0)
    col = lax.broadcasted_iota(jnp.int32, (ROWS, ROWS), 1)

    def natural(i):
        return ((i >> 2) & 3) * 32 + (i >> 4) * 4 + (i & 3)

    load_orig.wait()
    o = dot(jnp.where(col == natural(row), 1.0, 0.0).astype(BF16), orig[...])
    olog[...] = o
    eo[...] = jnp.exp(o)
    received(copies)
    for k in range(4):
        xf[4 * k : 4 * k + 4, 0:256] = zx[k, 0:4, :]
        xf[4 * k : 4 * k + 4, 256:512] = zx[k, 4:8, :]
    cols_q = block_of(piece, 512)
    rows_y = block_of(y, 16)
    xi[rows_y, cols_q] = xf[...].astype(BF16)
    block = xi.at[rows_y, cols_q]
    copies = {k: send(block, block, on_y(k)) for k in (4, 3, 5, 2, 6, 1, 7)}
    block = xi.at[:, cols_q]
    pieces = [group(on_x(k), block) for k in (1, 2, 3)]

    def forward_rows(k):
        here = xi.at[block_of(lax.rem(y - k + 8, 8), 16), cols_q]
        for start, _ in pieces:
            start(here)

    forward_rows(0)
    for k in (1, 7, 2, 6, 3, 5, 4):
        copies[k].wait_recv()
        forward_rows(k)
    forwards = [send(block, block, on_core())]
    for k in (1, 3, 2):
        pieces[k - 1][1].wait_recv()
        q = lax.rem(x - k + 4, 4) * 2 + core
        block = xi.at[:, block_of(q, 512)]
        forwards.append(send(block, block, on_core()))
    load_enc.wait()
    load_encb.wait()
    received(forwards)

    pre = encb[...]
    for j in range(7):
        cols = pl.ds(j * 512, 512)
        pre = pre + dot(xi[:, cols], enc[:, cols], NT)
    four = 4.0 * pre
    acts = (jnp.maximum(four, 0.0) + jnp.log1p(jnp.exp(-jnp.abs(four)))) * 0.25
    acts_ref[...] = acts.astype(BF16)
    sig[...] = jax.nn.sigmoid(four)
    load_dec.wait()
    load_gain.wait()
    load_unemb.wait()

    cols_z = block_of(z, 256)

    def all_reduce(r, left, right, core_out, core_in, xs, xr, zs, zr, ye, full, bias, early):
        def term(half, j):
            return dot(left, right[:, pl.ds(pl.multiple_of(half * HALF + j * 256, 256), 256)])

        copies = []
        for begin, end in ((0, 4), (4, 7)):
            for j in range(begin, end):
                core_out[r, :, pl.ds(j * 256, 256)] = term(other, j).astype(BF16)
            cols = pl.ds(begin * 256, (end - begin) * 256)
            copies.append(send(core_out.at[r, :, cols], core_in.at[r, :, cols], on_core()))
        yield
        out = []
        for (begin, end), copy in zip(((0, 4), (4, 7)), copies):
            copy.wait_recv()
            for j in range(begin, end):
                cols = pl.ds(j * 256, 256)
                s = term(core, j) + core_in[r, :, cols].astype(F32)
                p_own[r, :, cols] = s
                xs[r, :, cols] = s.astype(BF16)
            cols = pl.ds(begin * 256, (end - begin) * 256)
            for k in (2, 1, 3):
                there = block_of(lax.rem(x + k, 4), 16)
                out.append(send(xs.at[r, there, cols], xr.at[r, k - 1, :, cols], on_x(k)))
        copies = out
        yield
        received(copies)
        s = p_own[r, block_of(x, 16), :]
        for k in range(3):
            s = s + xr[r, k].astype(F32)
        acc[r, :, 0:HALF] = s
        zs[r, :, 0:HALF] = s.astype(BF16)
        copies = []
        for k in (4, 3, 5, 2, 6, 1, 7):
            there = block_of(lax.rem(z + k, 8), 256)
            copies.append(send(zs.at[r, :, there], zr.at[r, k - 1], on_z(k)))
        yield
        received(copies)
        s = acc[r, :, cols_z]
        for k in range(7):
            s = s + zr[r, k].astype(F32)
        ye[r, y] = s.astype(BF16)
        copies = [send(ye.at[r, y], ye.at[r, y], on_y(k)) for k in (4, 3, 5, 2, 6, 1, 7)]
        yield
        received(copies)
        s = ye[r, 0].astype(F32)
        for k in range(1, 8):
            s = s + ye[r, k].astype(F32)
        if bias is not None:
            begin = pl.multiple_of(core * HALF + jnp.minimum(z, 6) * 256, 256)
            s = s + bias[:, pl.ds(begin, 256)]
        rows_x = block_of(4 * r + x, 16)
        full[core, rows_x, cols_z] = s.astype(BF16)
        block = full.at[core, rows_x, cols_z]
        copies = {k: send(block, block, on_z(k)) for k in (4, 3, 5, 2, 6, 1, 7)}
        whole = full.at[core, rows_x, pl.ds(0, HALF)]
        pieces = [group(on_x(k), whole) for k in (1, 2, 3)]

        def forward_columns(k):
            owner = lax.rem(z - k + 8, 8)

            @pl.when(owner != 7)
            def _():
                for start, _ in pieces:
                    start(full.at[core, rows_x, block_of(owner, 256)])

        forward_columns(0)
        yield
        for first, second in ((1, 7), (2, 6)):
            copies[first].wait_recv()
            forward_columns(first)
            copies[second].wait_recv()
            forward_columns(second)
        yield
        for k in (3, 5, 4):
            copies[k].wait_recv()
            forward_columns(k)
        block = full.at[core, rows_x, pl.ds(0, HALF)]
        forwards = [send(block, block, on_core())]
        yield
        for k in (1, 3, 2):
            pieces[k - 1][1].wait_recv()
            here = block_of(4 * r + lax.rem(x - k + 4, 4), 16)
            block = full.at[core, here, pl.ds(0, HALF)]
            forwards.append(send(block, block, on_core()))
        early()
        yield
        received(forwards)

    def exchange(buffer, value, here, count, target):
        buffer[here] = value
        order = [k for k in (4, 3, 5, 2, 6, 1, 7) if k < count]
        copies = [send(buffer.at[here], buffer.at[here], target(k)) for k in order]
        yield
        received(copies)
        total = buffer[0]
        for k in range(1, count):
            total = total + buffer[k]
        return total

    kls = [None, None]
    dpres = [None, None]

    def chain(r):
        rows = pl.ds(r * CHAIN, CHAIN)
        squares = [jnp.zeros((CHAIN, 256), F32)]
        raw = [jnp.zeros((CHAIN, VOC), F32)]

        def logit_terms(half):
            for j in range(7):
                cols = pl.ds(pl.multiple_of(half * HALF + j * 256, 256), 256)
                v = xh[half, rows, pl.ds(j * 256, 256)].astype(F32)
                squares[0] = squares[0] + v * v
                raw[0] = raw[0] + dot((v * gain_ref[:, cols]).astype(BF16), unemb[:, cols], NT)

        yield from all_reduce(
            r, acts_ref[rows, :], dec, core_out, core_in, xs, xr, zs, zr, ye, xh, decb,
            lambda: logit_terms(core),
        )
        logit_terms(other)
        rinv = lax.rsqrt(jnp.sum(squares[0], axis=1, keepdims=True) * (1.0 / D) + 1e-06)
        raw = raw[0] * rinv
        shape = jnp.tanh(raw * (1.0 / 30.0))
        capped = 30.0 * shape
        exp_model = jnp.exp(capped)
        exp_orig = eo[rows, :]

        lane = lax.broadcasted_iota(jnp.int32, (CHAIN, ROWS), 1)
        sums = jnp.where(lane == 0, jnp.sum(exp_model, axis=1, keepdims=True), 0.0)
        sums = jnp.where(lane == 1, jnp.sum(exp_orig, axis=1, keepdims=True), sums)
        cross = jnp.sum(exp_orig * (olog[rows, :] - capped), axis=1, keepdims=True)
        sums = jnp.where(lane == 2, cross, sums)
        s = jnp.concatenate([sums, jnp.zeros((CHAIN, ROWS), F32)], axis=0).T[0:4, :]
        here = x * 2 + core
        slot = small_x.at[r, here]
        slot[...] = s
        copies = [send(slot, slot, on_xc(k, f)) for k in (2, 1, 3, 0) for f in (True, False) if k or f]
        yield
        received(copies)
        s = small_x[r, 0]
        for k in range(1, 8):
            s = s + small_x[r, k]
        s = yield from exchange(small_z.at[r], s, z, 8, on_z)
        s = yield from exchange(small_y.at[r], s, y, 8, on_y)
        kls[r] = s[2:3] / s[1:2] - jnp.log(s[1:2]) + jnp.log(s[0:1])
        columns = jnp.concatenate([s, jnp.zeros((ROWS - 4, ROWS), F32)], axis=0).T[0:CHAIN, :]
        dcap = exp_model * (1.0 / columns[:, 0:1]) - exp_orig * (1.0 / columns[:, 1:2])
        dz = (dcap * (1.0 - shape * shape)).astype(BF16)
        dots = [jnp.zeros((CHAIN, 256), F32)]

        def dot_terms(half):
            for j in range(7):
                cols = pl.ds(j * 256, 256)
                gain = gain_ref[:, pl.ds(pl.multiple_of(half * HALF + j * 256, 256), 256)]
                scaled = dn[half, rows, cols].astype(F32) * gain
                dots[0] = dots[0] + xh[half, rows, cols].astype(F32) * scaled

        yield from all_reduce(
            r, dz, unemb, core_out2, core_in2, xs2, xr2, zs2, zr2, ye2, dn, None,
            lambda: dot_terms(core),
        )
        dot_terms(other)
        factor = jnp.sum(dots[0], axis=1, keepdims=True) * (1.0 / D) * rinv * rinv
        back = jnp.zeros((CHAIN, LAT), F32)
        for half in range(2):
            for j in range(7):
                cols = pl.ds(j * 256, 256)
                whole = pl.ds(half * HALF + j * 256, 256)
                scaled = dn[half, rows, cols].astype(F32) * gain_ref[:, whole]
                dxhat = rinv * (scaled - xh[half, rows, cols].astype(F32) * factor)
                brow[r, :, whole] = jnp.sum(dxhat, axis=0, keepdims=True)
                rounded = dxhat.astype(BF16)
                dxl[rows, whole] = rounded
                back = back + dot(rounded, dec[:, whole], NT)
        dpres[r] = back * sig[rows, :]

    running = [chain(0), chain(1)]
    while running:
        for generator in list(running):
            try:
                next(generator)
            except StopIteration:
                running.remove(generator)

    dpre = jnp.concatenate(dpres, axis=0)
    ebg = jnp.sum(dpre, axis=0, keepdims=True)
    ebg_ref[...] = ebg

    high = ebg.astype(BF16).astype(F32)
    middle = (ebg - high).astype(BF16).astype(F32)
    last = ebg - high - middle
    stacked = jnp.concatenate([high, middle, last, jnp.zeros((13, LAT), F32)], axis=0).astype(BF16)
    for j in range(7):
        part = dot(stacked, enc[:, 512 * j : 512 * j + 512])
        th[j : j + 1, :] = part[0:1] + part[1:2] + part[2:3]
    th[7:8, :] = jnp.zeros((1, 512), F32)
    here, there = block_of(core, 256), block_of(other, 256)
    copy = send(th.at[:, there], th_c, on_core())
    acts_t = acts_ref[...].astype(F32).T.astype(BF16)
    dpre_t = dpre.T.astype(BF16)
    copy.wait_recv()

    stores = []
    n_sent = len(sent)

    def row_kl():
        rest = jnp.zeros((8, ROWS), F32)
        for r in range(2):
            perm = jnp.where((col == natural(row + CHAIN * r)) & (row < CHAIN), 1.0, 0.0)
            kl = jnp.where(lax.broadcasted_iota(jnp.int32, (8, ROWS), 1) < CHAIN, kls[r], 0.0)
            rest = rest + dot(kl, perm, precision=lax.Precision.HIGHEST)
        kl_ref[...] = rest
        stores.append(load(10, kl_ref.at[0], kl_hbm))
        stores.append(load(11, ebg_ref.at[0], ebg_hbm))

    def grad_dec():
        for j in range(7):
            cols = pl.ds(j * 512, 512)
            gdec[:, cols] = dot(acts_t, dxl[:, cols]).astype(BF16)
        stores.append(load(7, gdec, gdec_hbm))

    def grad_enc():
        for j in range(7):
            cols = pl.ds(j * 512, 512)
            genc[:, cols] = dot(dpre_t, xi[:, cols]).astype(BF16)
        stores.append(load(8, genc, genc_hbm))
        for copy in sent[:n_sent]:
            copy.wait_send()

    total = yield_through(exchange(th_x, th[:, here] + th_c[...], x, 4, on_x), row_kl)
    total = yield_through(exchange(th_z, total, z, 8, on_z), grad_dec)
    total = yield_through(exchange(th_y, total, y, 8, on_y), grad_enc)
    th_all[:, here] = total
    copy = send(th_all.at[:, here], th_all.at[:, here], on_core())
    copy.wait_recv()
    for j in range(7):
        cols = pl.ds(512 * j, 512)
        gbd_ref[:, cols] = brow[0, :, cols] + brow[1, :, cols] - th_all[j : j + 1, :]
    stores.append(load(12, gbd_ref.at[0], gbd_hbm))
    for copy in sent[n_sent:]:
        copy.wait_send()
    for store in stores:
        store.wait()


def yield_through(generator, meanwhile):
    next(generator)
    meanwhile()
    try:
        next(generator)
    except StopIteration as end:
        return end.value


def copy_out(*refs):
    ins, outs, held, sems = refs[0:5], refs[5:10], refs[10:15], refs[15]

    def views(refs):
        return [ref.at[0] if len(ref.shape) == 2 and ref.shape[0] == 1 else ref for ref in refs]

    held = views(held)
    loads = [pltpu.make_async_copy(ins[i], held[i], sems.at[0, i]) for i in range(5)]
    stores = [pltpu.make_async_copy(held[i], outs[i], sems.at[1, i]) for i in range(5)]
    for copy in loads:
        copy.start()
    for load, store in zip(loads, stores):
        load.wait()
        store.start()
    for copy in stores:
        copy.wait()


def per_device(resid, enc_weight, enc_bias, dec_weight, dec_bias, norm_gain, unembed, orig_logits):
    hbm = pl.BlockSpec(memory_space=pl.ANY)
    reduce_scratch = [
        pltpu.VMEM((2, CHAIN, HALF), BF16),
        pltpu.VMEM((2, CHAIN, HALF), BF16),
        pltpu.VMEM((2, CHAIN, HALF), BF16),
        pltpu.VMEM((2, 3, 16, HALF), BF16),
        pltpu.VMEM((2, 16, 2048), BF16),
        pltpu.VMEM((2, 7, 16, 256), BF16),
        pltpu.VMEM((2, 8, 16, 256), BF16),
        pltpu.VMEM((2, ROWS, 2048), BF16),
    ]
    shapes = (
        jax.ShapeDtypeStruct((LAT, D), BF16),
        jax.ShapeDtypeStruct((LAT, D), BF16),
        jax.ShapeDtypeStruct((LAT,), F32),
        jax.ShapeDtypeStruct((D,), F32),
        jax.ShapeDtypeStruct((ROWS,), F32),
    )
    results = pl.pallas_call(
        kernel,
        out_shape=shapes,
        in_specs=[hbm] * 8,
        out_specs=(hbm,) * 5,
        scratch_shapes=[
            pltpu.VMEM((4, D), BF16),
            pltpu.VMEM((1, LAT), F32),
            pltpu.VMEM((1, D), F32),
            pltpu.VMEM((8, ROWS), F32),
            pltpu.VMEM((LAT, D), BF16),
            pltpu.VMEM((LAT, D), BF16),
            pltpu.VMEM((VOC, D), BF16),
            pltpu.VMEM((1, LAT), F32),
            pltpu.VMEM((1, D), F32),
            pltpu.VMEM((1, D), F32),
            pltpu.VMEM((ROWS, VOC), BF16),
            pltpu.VMEM((LAT, D), BF16),
            pltpu.VMEM((LAT, D), BF16),
            pltpu.VMEM((4, 8, 256), F32),
            pltpu.VMEM((16, 512), F32),
            pltpu.VMEM((ROWS, 4096), BF16),
            pltpu.VMEM((2, CHAIN, HALF), F32),
            pltpu.VMEM((2, 16, 2048), F32),
            *reduce_scratch,
            *reduce_scratch,
            pltpu.VMEM((ROWS, VOC), F32),
            pltpu.VMEM((ROWS, VOC), F32),
            pltpu.VMEM((ROWS, LAT), F32),
            pltpu.VMEM((ROWS, LAT), BF16),
            pltpu.VMEM((ROWS, D), BF16),
            pltpu.VMEM((2, 1, D), F32),
            *(pltpu.VMEM((2, 8, 4, ROWS), F32) for _ in range(3)),
            pltpu.VMEM((8, 512), F32),
            pltpu.VMEM((8, 256), F32),
            *(pltpu.VMEM((n, 8, 256), F32) for n in (4, 8, 8)),
            pltpu.VMEM((8, 512), F32),
            pltpu.SemaphoreType.DMA((13,)),
            pltpu.SemaphoreType.DMA((N_SEMS,)),
            pltpu.SemaphoreType.DMA((N_SEMS,)),
        ],
        compiler_params=pltpu.CompilerParams(
            collective_id=0, has_side_effects=True, vmem_limit_bytes=60 * 2**20
        ),
        cost_estimate=pl.CostEstimate(flops=10**9, bytes_accessed=5 * 10**6, transcendentals=0),
        name="train_step",
    )(resid, enc_weight, enc_bias, dec_weight, dec_bias, norm_gain, unembed, orig_logits)
    return pl.pallas_call(
        copy_out,
        out_shape=shapes,
        in_specs=[hbm] * 5,
        out_specs=(hbm,) * 5,
        scratch_shapes=[
            pltpu.VMEM((LAT, D), BF16),
            pltpu.VMEM((LAT, D), BF16),
            pltpu.VMEM((1, LAT), F32),
            pltpu.VMEM((1, D), F32),
            pltpu.VMEM((1, ROWS), F32),
            pltpu.SemaphoreType.DMA((2, 5)),
        ],
        compiler_params=pltpu.CompilerParams(vmem_limit_bytes=60 * 2**20),
        name="copy_out",
    )(*results)


def solution(mesh):
    split = P(("tok", "lat"), None)
    return jax.shard_map(
        per_device,
        mesh=mesh,
        in_specs=(
            P("tok", None), split, P(("tok", "lat")), split, P(), P(), split,
            P(None, ("tok", "lat")),
        ),
        out_specs=(split, split, P(("tok", "lat")), P(), P()),
        check_vma=False,
    )
```
